256 devices in a mesh: pair: 64 (over z, y, core), vec: 4 (over x).
Axes of the slice: x: 4, y: 4, z: 8, core: 2. Of those that a mesh axis runs over, the one named last changes fastest.
Arguments:
- vectors: float32 [262144, 1536], P(('pair', 'vec')), may hold values from -1 to 1
- columns: float32 [2, 262144, 256], P(None, ('pair', 'vec')), may hold values from -6 to 6
- inverse_factor: float32 [2, 256, 256], replicated, as said below
- diagonal: float32 [262144], P(('pair', 'vec')), may hold values from 4 to 12
- pivots: int32 [2, 256], replicated, may hold values from 0 to 262143, as said below
- shell_map: int32 [262144], P(('pair', 'vec')), may hold values from 0 to 16383
Outputs:
- relaid: float32 [512, 262144], P(('pair', 'vec'))
- diagonal_out: float32 [262144], P(('pair', 'vec'))
- shell_sums: float32 [16384], P(('pair', 'vec'))
The draws below stay inside these ranges and needn't reach their ends.
Inputs may be any that keep to these rules, and one draw needn't show every extreme that they name: The 256 pivots of batch b are different rows of one shard, the owner o_b: all within o_b * 1024 to (o_b + 1) * 1024 - 1; the two batches have different owners, one of which is the last shard; each batch includes its owner's last row. Each inverse_factor[b] is upper triangular with a positive diagonal.
All inputs are finite; a program needn't handle non-finite values.
Results may differ from the reference program's by a relative error of at most 0.00007.
Values sent between devices are 32-bit elements; how exact they have to be, the bound alone decides.
A program may use at most 64 MiB of HBM per device.

```python
import jax
import jax.numpy as jnp
from jax import lax

RANK = 1536
B = 256
ROWS_DEV = 1024
ROWS = 262144
NSP = 16384


def owner_pair(key):
    shards = ROWS // ROWS_DEV
    other = jax.random.randint(jax.random.fold_in(key, 11), (), 0, shards - 1)
    flip = jax.random.randint(jax.random.fold_in(key, 12), (), 0, 2)
    last = jnp.int32(shards - 1)
    first = jnp.where(flip == 1, other, last)
    second = jnp.where(flip == 1, last, other)
    return jnp.stack([first, second]).astype(jnp.int32)


def batch_rows(key, index):
    chosen = jax.random.permutation(jax.random.fold_in(key, index), ROWS_DEV - 1)[:B - 1].astype(jnp.int32)
    full = jnp.concatenate([chosen, jnp.full((1,), ROWS_DEV - 1, jnp.int32)])
    order = jax.random.permutation(jax.random.fold_in(key, index + 10), B)
    return full[order]


def draw_pivots(key, part):
    owners = owner_pair(key)
    key = jax.random.fold_in(key, 3)
    local = jnp.stack([batch_rows(key, 0), batch_rows(key, 1)]).astype(jnp.int32)
    return local + owners[:, None] * ROWS_DEV


def draw_inverse_factor(key, part):
    key = jax.random.fold_in(key, 5)
    key_diag, key_off = jax.random.split(key)
    diag_values = jax.random.uniform(key_diag, (2, B), jnp.float32, 0.03, 0.06)
    off_values = 0.004 * jax.random.normal(key_off, (2, B, B), jnp.float32)
    row_index = lax.broadcasted_iota(jnp.int32, (B, B), 0)
    col_index = lax.broadcasted_iota(jnp.int32, (B, B), 1)
    upper = jnp.where(col_index > row_index, off_values, 0.0)
    return upper + jnp.where(col_index == row_index, diag_values[:, :, None], 0.0)


def plant(values, stream_key, low, top_value):
    index_at = [jax.random.randint(jax.random.fold_in(stream_key, axis), (), 0, length) for axis, length in enumerate(values.shape)]
    widest = values.shape.index(max(values.shape))
    beside = index_at[:widest] + [(index_at[widest] + 1) % values.shape[widest]] + index_at[widest + 1:]
    return values.at[tuple(index_at)].set(low).at[tuple(beside)].set(top_value)


def level_of(rng, dims, cuts, least, top_value):
    gain = 1.0
    for axis_at, blocks in cuts:
        draws = jax.random.uniform(jax.random.fold_in(jax.random.fold_in(rng, 6), axis_at), (blocks,), jnp.float32, least / len(cuts), top_value / len(cuts))
        gain = gain * jnp.repeat(jnp.exp(draws), dims[axis_at] // blocks).reshape((-1,) + (1,) * (len(dims) - 1 - axis_at))
    return gain


def scatter_about(stream_key, shape, scale, bound, pieces=(), held_as=jnp.bfloat16):
    drawn = jax.random.normal(stream_key, shape, jnp.float32) * scale
    if len(pieces) > 0:
        drawn = level_of(stream_key, shape, pieces, -0.22, 0.18) * drawn
    return jnp.clip(drawn, min=-bound, max=bound).astype(held_as)


def setup_inputs(seed: int = 0) -> dict:
    key_list = jax.random.split(jax.random.key(seed), 7)
    vectors = scatter_about(key_list[0], (ROWS, RANK), 0.16, 1.0, ((0, 256),), jnp.float32)
    columns = scatter_about(key_list[1], (2, ROWS, B), 1.0, 6.0, ((1, 256),), jnp.float32)
    inverse_factor = draw_inverse_factor(jax.random.fold_in(key_list[6], 71), 0)
    diagonal = jnp.clip(4.0 + 8.0 * jax.random.uniform(key_list[3], (ROWS,), jnp.float32) ** level_of(key_list[3], (ROWS,), ((0, 256),), -0.2, 0.2), 4.0, 12.0)
    pivots = draw_pivots(jax.random.fold_in(key_list[6], 71), 0)
    shell_map = plant(jax.random.randint(key_list[5], (ROWS,), 0, NSP), jax.random.fold_in(key_list[5], 1), 0, NSP - 1).astype(jnp.int32)
    return dict(vectors=vectors, columns=columns, inverse_factor=inverse_factor, diagonal=diagonal, pivots=pivots, shell_map=shell_map)


def contract(left, right, left_dim, right_dim):
    return lax.dot_general(left, right, (((left_dim,), (right_dim,)), ((), ())), precision=lax.Precision.HIGHEST, preferred_element_type=jnp.float32)


def reference(vectors, columns, inverse_factor, diagonal, pivots, shell_map):
    pivot_first = vectors[pivots[0]]
    resid_first = columns[0] - contract(vectors, pivot_first, 1, 1)
    new_first = contract(resid_first, inverse_factor[0], 1, 0)
    pivot_old = vectors[pivots[1]]
    pivot_new = new_first[pivots[1]]
    resid_second = columns[1] - contract(vectors, pivot_old, 1, 1) - contract(new_first, pivot_new, 1, 1)
    new_second = contract(resid_second, inverse_factor[1], 1, 0)
    relaid = jnp.concatenate([new_first, new_second], axis=1).T
    diagonal_out = diagonal - jnp.sum(new_first * new_first, axis=1) - jnp.sum(new_second * new_second, axis=1)
    shell_sums = jax.ops.segment_sum(diagonal_out, shell_map, num_segments=NSP)
    return relaid, diagonal_out, shell_sums
```

```python
import functools

import jax
import jax.numpy as jnp
from jax import lax
from jax.experimental import pallas as pl
from jax.experimental.pallas import tpu as pltpu
from jax.sharding import PartitionSpec as P

NSP_DEV = 64


def from_root(shard, axis, root):
    mine = lax.axis_index(axis) == root
    return lax.psum(jnp.where(mine, shard, jnp.zeros_like(shard)), axis)


def contract(left, right, left_dim, right_dim):
    return lax.dot_general(
        left,
        right,
        (((left_dim,), (right_dim,)), ((), ())),
        precision=lax.Precision.HIGHEST,
        preferred_element_type=jnp.float32,
    )


def exchange_kernel(npair, nvec, new_ref, out_ref, send_sem, recv_sem):
    pair = lax.axis_index("pair")
    vec = lax.axis_index("vec")
    devices, _, rows = new_ref.shape
    me = pair * nvec + vec
    here = out_ref.at[:, pl.ds(pl.multiple_of(me * rows, rows), rows)]
    pltpu.make_async_copy(new_ref.at[me], here, recv_sem).start()

    def send(step, carry):
        to_pair = lax.rem(pair + lax.rem(step, 8) * 8 + lax.div(lax.rem(step, 64), 8), npair)
        to_vec = lax.rem(vec + lax.div(step, 64), nvec)
        pltpu.make_async_remote_copy(
            src_ref=new_ref.at[to_pair * nvec + to_vec],
            dst_ref=here,
            send_sem=send_sem,
            recv_sem=recv_sem,
            device_id=(to_pair, to_vec),
            device_id_type=pl.DeviceIdType.MESH,
        ).start()
        return carry

    lax.fori_loop(1, devices, send, 0)
    pltpu.make_async_copy(out_ref, out_ref, recv_sem).wait()
    sent = new_ref.at[pl.ds(0, devices - 1)]
    pltpu.make_async_copy(sent, sent, send_sem).wait()


def exchange(new):
    npair = lax.axis_size("pair")
    nvec = lax.axis_size("vec")
    devices, per_device, rows = new.shape
    return pl.pallas_call(
        functools.partial(exchange_kernel, npair, nvec),
        out_shape=jax.ShapeDtypeStruct((per_device, devices * rows), jnp.float32),
        in_specs=[pl.BlockSpec(memory_space=pl.ANY)],
        out_specs=pl.BlockSpec(memory_space=pl.ANY),
        scratch_shapes=[pltpu.SemaphoreType.DMA, pltpu.SemaphoreType.DMA],
        compiler_params=pltpu.CompilerParams(has_side_effects=True),
        name="exchange",
    )(new)


def on_device(vectors, columns, inverse_factor, diagonal, pivots, shell_map):
    rows_dev = vectors.shape[0]
    batch = inverse_factor.shape[1]
    npair = lax.axis_size("pair")
    nvec = lax.axis_size("vec")
    per_device = 2 * batch // (npair * nvec)
    factor_first = inverse_factor[0]
    factor_second = inverse_factor[1]
    owner_first = pivots[0, 0] // rows_dev
    owner_second = pivots[1, 0] // rows_dev
    local_first = pivots[0] - owner_first * rows_dev
    local_second = pivots[1] - owner_second * rows_dev
    picked_first = jnp.take(vectors, local_first, axis=0, mode="clip")
    rows_first = from_root(picked_first, ("pair", "vec"), owner_first)
    resid_first = columns[0] - contract(vectors, rows_first, 1, 1)
    new_first = contract(factor_first, resid_first, 0, 1)
    picked_new = jnp.take(new_first, local_second, axis=1, mode="clip").T
    picked_both = jnp.concatenate(
        [jnp.take(vectors, local_second, axis=0, mode="clip"), picked_new], axis=1
    )
    rows_both = from_root(picked_both, ("pair", "vec"), owner_second)
    rows_old = rows_both[:, : vectors.shape[1]]
    rows_new = rows_both[:, vectors.shape[1] :]
    resid_second = (
        columns[1] - contract(vectors, rows_old, 1, 1) - contract(new_first, rows_new, 0, 1)
    )
    new_second = contract(factor_second, resid_second, 0, 1)
    diagonal_out = (
        diagonal - jnp.sum(new_first * new_first, axis=0) - jnp.sum(new_second * new_second, axis=0)
    )
    stacked = jnp.concatenate([new_first, new_second], axis=0)
    relaid = exchange(stacked.reshape(npair * nvec, per_device, rows_dev))
    shell_count = NSP_DEV * npair * nvec
    local_sums = jax.ops.segment_sum(diagonal_out, shell_map, num_segments=shell_count)
    shell_sums = lax.psum_scatter(local_sums, ("pair", "vec"), scatter_dimension=0, tiled=True)
    return (relaid, diagonal_out, shell_sums)


def solution(mesh):
    in_specs = (
        P(("pair", "vec"), None),
        P(None, ("pair", "vec"), None),
        P(),
        P(("pair", "vec")),
        P(),
        P(("pair", "vec")),
    )
    out_specs = (P(("pair", "vec"), None), P(("pair", "vec")), P(("pair", "vec")))
    return jax.shard_map(
        on_device, mesh=mesh, in_specs=in_specs, out_specs=out_specs, check_vma=False
    )
```

```python
import functools

import jax
import jax.numpy as jnp
from jax import lax
from jax.experimental import pallas as pl
from jax.experimental.pallas import tpu as pltpu
from jax.sharding import PartitionSpec as P

F32 = jnp.float32
BF16 = jnp.bfloat16
MESH = pl.DeviceIdType.MESH

NZ, NY, NX, NC = 8, 4, 4, 2
BATCH = 256
RANK = 1536
ROWS = 1024
DEVICES = NZ * NY * NX * NC
SHELLS = 64
BLOCK = 512

LOW = (0, 512, 128)
HIGH = (1024, 384, 128)
WIDE = RANK + BATCH
LAST = (0, 768, 1536)


def split(x):
    high = x.astype(BF16)
    return high, (x - high.astype(F32)).astype(BF16)


def dot_nn(a, b):
    return lax.dot_general(a, b, (((1,), (0,)), ((), ())), preferred_element_type=F32)


def dot_nt(a, b):
    return lax.dot_general(a, b, (((1,), (1,)), ((), ())), preferred_element_type=F32)


def three(dot, a, b):
    return dot(a[0], b[0]) + (dot(a[0], b[1]) + dot(a[1], b[0]))


def times(i, n):
    return pl.multiple_of(i * n, n)


class Group:
    def __init__(self, spec, refs):
        self.first, self.width, self.part = spec
        (self.r0, self.h, self.r1a, self.r1b, self.h2a, self.h2b, self.r2a, self.r2b,
         self.g, self.r3, self.g2, self.send, self.recv) = refs


def group_scratch(spec):
    _, width, part = spec
    return [
        pltpu.VMEM((BATCH, width), F32),
        pltpu.VMEM((BATCH, width), F32),
        pltpu.VMEM((3, 32, width), F32),
        pltpu.VMEM((3, 32, width), F32),
        pltpu.VMEM((32, width), F32),
        pltpu.VMEM((32, width), F32),
        pltpu.VMEM((3, 8, width), F32),
        pltpu.VMEM((3, 8, width), F32),
        pltpu.VMEM((8, 2 * width), F32),
        pltpu.VMEM((NZ - 1, 8, part), F32),
        pltpu.VMEM((8, 2 * width), F32),
        pltpu.SemaphoreType.DMA((12,)),
        pltpu.SemaphoreType.DMA((16,)),
    ]


def last_scratch(spec):
    _, width, _ = spec
    return [
        pltpu.VMEM((8, 2 * width), F32),
        pltpu.SemaphoreType.DMA((12,)),
        pltpu.SemaphoreType.DMA((16,)),
    ]


def kernel(
    vectors, columns, factor, diagonal, pivots, shells,
    relaid, diagonal_out, sums_out,
    v32, vh, vl, c32, pick, pick_last, pa, pb, pah, pal, pbh, pbl, ya, yb,
    new, sums, arrived, load_sem, exchange_send, exchange_recv, sums_send, sums_recv,
    *group_refs,
):
    pair = lax.axis_index("pair")
    x = lax.axis_index("vec")
    z, y, c = pair // (NY * NC), (pair // NC) % NY, pair % NC
    me = pair * NX + x
    n = len(group_scratch(LOW))
    low, high = Group(LOW, group_refs[:n]), Group(HIGH, group_refs[n : 2 * n])
    g2_last, last_send, last_recv = group_refs[2 * n :]

    def at(z=z, y=y, x=x, c=c):
        return ((z * NY + y) * NC + c, x)

    def along_x(d):
        return (x + d) % NX

    def along_y(d):
        return (y + d) % NY

    def along_z(d):
        return (z + d) % NZ

    def push(src, dst, send_sem, recv_sem, device):
        pltpu.make_async_remote_copy(
            src_ref=src, dst_ref=dst, send_sem=send_sem, recv_sem=recv_sem,
            device_id=device, device_id_type=MESH,
        ).start()

    def take(ref, sem):
        pltpu.make_async_copy(ref, ref, sem).wait()

    def load(i, width=256):
        at_cols = pl.ds(times(i, width), width)
        return pltpu.make_async_copy(vectors.at[:, at_cols], v32.at[:, at_cols], load_sem.at[i])

    order = [(1 - c) * 2, (1 - c) * 2 + 1, c * 2, c * 2 + 1, 4, 5]
    for i in order:
        load(i).start()
    load_columns = pltpu.make_async_copy(columns, c32, load_sem.at[6])
    load_columns.start()

    barrier = pltpu.get_barrier_semaphore()

    def greet(device):
        pl.semaphore_signal(barrier, inc=1, device_id=device, device_id_type=MESH)

    greet(at(c=1 - c))
    for d in range(1, 4):
        greet(at(x=along_x(d)))
        greet(at(y=along_y(d)))
    for d in range(1, NZ):
        greet(at(z=along_z(d)))
    root = me == DEVICES - 1
    apart = (x != NX - 1).astype(jnp.int32) + (y != NY - 1).astype(jnp.int32) + (c != NC - 1).astype(jnp.int32)

    @pl.when((z == NZ - 1) & (apart >= 2))
    def _():
        greet(at(z=NZ - 1, y=NY - 1, x=NX - 1, c=NC - 1))

    eye = lax.broadcasted_iota(jnp.int32, (BATCH, BATCH), 0) == lax.broadcasted_iota(jnp.int32, (BATCH, BATCH), 1)
    row = lax.broadcasted_iota(jnp.int32, (BATCH, ROWS), 1) + me * ROWS
    hot = [
        row == jnp.sum(jnp.where(eye, pivots[b : b + 1, :], 0), axis=1, keepdims=True)
        for b in range(2)
    ]
    hot_second = jnp.where(hot[1], 1.0, 0.0).astype(BF16)
    hot_any = jnp.where(hot[0] | hot[1], 1.0, 0.0).astype(BF16)
    kept = jnp.where(root, 0.0, 1.0).astype(F32)

    def gather(i):
        at_cols = pl.ds(times(i, 256), 256)
        load(i).wait()
        vh[:, at_cols], vl[:, at_cols] = split(v32[:, at_cols])
        rows = dot_nn(hot_any, vh[:, at_cols]) + dot_nn(hot_any, vl[:, at_cols])
        pick_last[:, at_cols] = rows
        pick[:, at_cols] = rows * kept

    def half(first, width, core):
        return pl.ds(pl.multiple_of(first + core * width, 128), width)

    def spread(p, g2, first, width, send, recv):
        mine = half(first, width, c)
        rows_a = pl.ds(times(x * NY + y, 8), 8)
        rows_b = pl.ds(pl.multiple_of(128 + (y * NX + x) * 8, 8), 8)
        p[rows_a, mine] = g2[:, :width]
        p[rows_b, mine] = g2[:, width:]
        for d in range(1, 4):
            push(g2.at[:, pl.ds(0, width)], p.at[rows_a, mine], send.at[6], recv.at[6], at(y=along_y(d)))
            push(g2.at[:, pl.ds(width, width)], p.at[rows_b, mine], send.at[6], recv.at[7], at(x=along_x(d)))
        yield
        three_rows = p.at[pl.ds(0, 24), pl.ds(0, width)]
        block_a = p.at[pl.ds(times(x, 32), 32), mine]
        block_b = p.at[pl.ds(pl.multiple_of(128 + y * 32, 32), 32), mine]
        take(three_rows, recv.at[6])
        for d in range(1, 4):
            push(block_a, block_a, send.at[7], recv.at[7 + d], at(x=along_x(d)))
        push(block_a, block_a, send.at[8], recv.at[14], at(c=1 - c))
        take(three_rows, recv.at[7])
        for d in range(1, 4):
            push(block_b, block_b, send.at[7], recv.at[10 + d], at(y=along_y(d)))
        push(block_b, block_b, send.at[8], recv.at[14], at(c=1 - c))
        yield
        for d in range(1, 4):
            block = p.at[pl.ds(times(along_x(4 - d), 32), 32), mine]
            take(block, recv.at[7 + d])
            push(block, block, send.at[8], recv.at[14], at(c=1 - c))
            block = p.at[pl.ds(pl.multiple_of(128 + along_y(4 - d) * 32, 32), 32), mine]
            take(block, recv.at[10 + d])
            push(block, block, send.at[8], recv.at[14], at(c=1 - c))
        yield
        take(p.at[:, pl.ds(0, width)], recv.at[14])

    def spread_sent(p, width, send):
        take(p.at[pl.ds(0, 48), pl.ds(0, width)], send.at[6])
        take(p.at[pl.ds(0, 192), pl.ds(0, width)], send.at[7])
        take(p.at[:, pl.ds(0, width)], send.at[8])

    def reduce(s):
        width, part, send, recv = s.width, s.part, s.send, s.recv
        parts = 2 * width // part
        push(pick.at[:, half(s.first, width, 1 - c)], s.r0, send.at[0], recv.at[0], at(c=1 - c))
        yield
        take(s.r0, recv.at[0])
        s.h[...] = pick[:, half(s.first, width, c)] + s.r0[...]
        for d in range(1, 4):
            to = along_x(d)
            push(s.h.at[pl.ds(times(to, 32), 32)], s.r1a.at[d - 1], send.at[1], recv.at[1], at(x=to))
            to = along_y(d)
            push(s.h.at[pl.ds(pl.multiple_of(128 + to * 32, 32), 32)], s.r1b.at[d - 1], send.at[1], recv.at[2], at(y=to))
        yield
        take(s.r1a, recv.at[1])
        s.h2a[...] = (s.h[pl.ds(times(x, 32), 32), :] + s.r1a[0]) + (s.r1a[1] + s.r1a[2])
        for d in range(1, 4):
            to = along_y(d)
            push(s.h2a.at[pl.ds(times(to, 8), 8)], s.r2a.at[d - 1], send.at[2], recv.at[3], at(y=to))
        take(s.r1b, recv.at[2])
        s.h2b[...] = (s.h[pl.ds(pl.multiple_of(128 + y * 32, 32), 32), :] + s.r1b[0]) + (s.r1b[1] + s.r1b[2])
        for d in range(1, 4):
            to = along_x(d)
            push(s.h2b.at[pl.ds(times(to, 8), 8)], s.r2b.at[d - 1], send.at[2], recv.at[4], at(x=to))
        yield
        take(s.r2a, recv.at[3])
        s.g[:, :width] = (s.h2a[pl.ds(times(y, 8), 8), :] + s.r2a[0]) + (s.r2a[1] + s.r2a[2])
        take(s.r2b, recv.at[4])
        s.g[:, width:] = (s.h2b[pl.ds(times(x, 8), 8), :] + s.r2b[0]) + (s.r2b[1] + s.r2b[2])
        for d in range(1, NZ):
            to = along_z(d)

            @pl.when(to < parts)
            def _():
                push(s.g.at[:, pl.ds(times(to, part), part)], s.r3.at[d - 1], send.at[3], recv.at[5], at(z=to))

        yield
        mine = pl.ds(times(z, part), part)

        @pl.when(z < parts)
        def _():
            take(s.r3, recv.at[5])
            total = s.g[:, mine]
            for d in range(1, NZ):
                total = total + s.r3[d - 1]
            s.g2[:, mine] = total
            for d in range(1, NZ):
                push(s.g2.at[:, mine], s.g2.at[:, mine], send.at[4], recv.at[15], at(z=along_z(d)))

        yield

        @pl.when(z < parts)
        def _():
            take(s.g2.at[:, pl.ds(0, (parts - 1) * part)], recv.at[15])

        @pl.when(z >= parts)
        def _():
            take(s.g2.at[:, pl.ds(0, parts * part)], recv.at[15])

        yield from spread(pa, s.g2, s.first, width, send, recv)

    def reduce_sent(s):
        width, part, send = s.width, s.part, s.send
        parts = 2 * width // part
        take(s.r0, send.at[0])
        take(s.h.at[pl.ds(0, 192)], send.at[1])
        take(s.h.at[pl.ds(0, 48)], send.at[2])

        @pl.when(z < parts)
        def _():
            take(s.g2.at[:, pl.ds(0, (parts - 1) * part)], send.at[3])
            take(s.r3, send.at[4])

        @pl.when(z >= parts)
        def _():
            take(s.g2.at[:, pl.ds(0, parts * part)], send.at[3])

        spread_sent(pa, width, send)

    def from_last():
        first, width, _ = LAST

        @pl.when(root)
        def _():
            def rows_of(y, x, c):
                cols = half(first, width, c)
                return (
                    pick_last.at[pl.ds(times(x * NY + y, 8), 8), cols],
                    pick_last.at[pl.ds(pl.multiple_of(128 + (y * NX + x) * 8, 8), 8), cols],
                )

            for part, src in enumerate(rows_of(y, x, c)):
                g2_last[:, part * width : (part + 1) * width] = src[...]

            def send_to(k, carry):
                y_to, x_to, c_to = (y + k // 2) % NY, (x + k // 8) % NX, (c + k) % NC
                for part, src in enumerate(rows_of(y_to, x_to, c_to)):
                    push(src, g2_last.at[:, pl.ds(part * width, width)], last_send.at[0], last_recv.at[0],
                         at(y=y_to, x=x_to, c=c_to))
                return carry

            lax.fori_loop(1, NY * NX * NC, send_to, 0)

        yield

        @pl.when((z == NZ - 1) & jnp.logical_not(root))
        def _():
            take(g2_last, last_recv.at[0])

        @pl.when(z == NZ - 1)
        def _():
            for d in range(1, NZ):
                push(g2_last, g2_last, last_send.at[1], last_recv.at[1], at(z=along_z(d)))

        yield

        @pl.when(z != NZ - 1)
        def _():
            take(g2_last, last_recv.at[1])

        yield from spread(pb, g2_last, first, width, last_send, last_recv)

    def from_last_sent():
        _, width, _ = LAST

        @pl.when(root)
        def _():
            take(pick_last.at[pl.ds(0, 248)], last_send.at[0])

        @pl.when(z == NZ - 1)
        def _():
            take(pick_last.at[pl.ds(0, 56)], last_send.at[1])

        spread_sent(pb, width, last_send)

    for i in order[:4]:
        gather(i)

    @pl.when(root)
    def _():
        pl.semaphore_wait(barrier, 38)

    @pl.when(jnp.logical_not(root))
    def _():
        pl.semaphore_wait(barrier, 14)

    a, b, last = reduce(low), reduce(high), from_last()

    def go(*streams):
        for stream in streams:
            next(stream, None)

    go(a)
    gather(order[4])
    gather(order[5])
    load_columns.wait()
    own = split(c32[0])
    pick[:, RANK:] = dot_nn(hot_second, own[0]) + dot_nn(hot_second, own[1])
    go(b, last)
    go(a, b, a, b, last, a, b, last, a, b, last, a, b, last, a, b, last)

    pbh[...], pbl[...] = split(pb[...])

    def times_last(i, carry):
        rows = pl.ds(times(i, 256), 256)
        yb[rows, :] = three(dot_nt, (vh[rows, :], vl[rows, :]), (pbh[...], pbl[...]))
        return carry

    lax.fori_loop(0, ROWS // 256, times_last, 0)
    go(a, b, a, b)

    f0, f1 = factor[0], factor[1]
    pah[...], pal[...] = split(pa[:, :RANK])
    cross = three(dot_nt, (pah[...], pal[...]), (pbh[...], pbl[...]))
    last_first = jnp.broadcast_to(pivots[0:1, 0:1], (BATCH, BATCH)) >= (DEVICES - 1) * ROWS
    cross = jnp.where(last_first, cross, cross.T)
    f0_parts = split(f0)
    pivot_new = three(dot_nn, split(pa[:, RANK:] - cross), f0_parts)
    onto = split(three(dot_nt, f0_parts, split(pivot_new)))
    f0_t, f1_t = split(f0.T), split(f1.T)
    last_first = jnp.broadcast_to(pivots[0:1, 0:1], (BLOCK, BATCH)) >= (DEVICES - 1) * ROWS

    def times_other(i, carry):
        rows = pl.ds(times(i, 256), 256)
        ya[rows, :] = three(dot_nt, (vh[rows, :], vl[rows, :]), (pah[...], pal[...]))
        return carry

    lax.fori_loop(0, ROWS // 256, times_other, 0)

    kinds = DEVICES // 2
    for block in range(ROWS // BLOCK):
        rows = pl.ds(block * BLOCK, BLOCK)
        y_a, y_b = ya[rows, :], yb[rows, :]
        resid = c32[0, rows, :] - jnp.where(last_first, y_b, y_a)
        parts = split(resid)
        new_first = three(dot_nt, f0_t, parts)
        resid = c32[1, rows, :] - jnp.where(last_first, y_a, y_b) - three(dot_nn, parts, onto)
        new_second = three(dot_nt, f1_t, split(resid))
        new[:kinds, :, rows] = new_first.reshape(kinds, 2, BLOCK)
        new[kinds:, :, rows] = new_second.reshape(kinds, 2, BLOCK)
        diagonal_out[:, rows] = diagonal[:, rows] - jnp.sum(
            new_first * new_first + new_second * new_second, axis=0, keepdims=True
        )
        here = relaid.at[:, pl.ds(pl.multiple_of(me * ROWS + block * BLOCK, BLOCK), BLOCK)]

        def send_new(k, carry):
            y_to, x_to, c_to = (y + k // 4) % NY, (x + k // 16) % NX, (c + k // 64) % NC
            for batch in range(2):
                z_to = batch * (NZ // 2) + (z + k) % (NZ // 2)
                pair_to, x_to = at(z=z_to, y=y_to, x=x_to, c=c_to)
                to = pair_to * NX + x_to
                src = new.at[to, :, rows]

                @pl.when(to == me)
                def _():
                    pltpu.make_async_copy(src, here, exchange_recv).start()

                @pl.when(to != me)
                def _():
                    push(src, here, exchange_send, exchange_recv, (pair_to, x_to))

            return carry

        lax.fori_loop(0, kinds, send_new, 0)

    shell = shells[...]
    hot_device = jnp.where(
        lax.broadcasted_iota(jnp.int32, (DEVICES, ROWS), 0) == shell // SHELLS, 1.0, 0.0
    ).astype(BF16)
    values = jnp.where(
        lax.broadcasted_iota(jnp.int32, (128, ROWS), 0) == shell % SHELLS, diagonal_out[...], 0.0
    )
    first, rest = values.astype(BF16), values
    rest = rest - first.astype(F32)
    second, third = split(rest)
    total = dot_nt(hot_device, first) + (dot_nt(hot_device, second) + dot_nt(hot_device, third))
    sums[...] = total.reshape(DEVICES, 1, 128)
    pltpu.make_async_copy(sums.at[me], arrived.at[me], sums_recv).start()

    def send_sums(k, carry):
        z_to, y_to, x_to, c_to = along_z(k), (y + k // 8) % NY, (x + k // 32) % NX, (c + k // 128) % NC
        pair_to, x_to = at(z=z_to, y=y_to, x=x_to, c=c_to)
        push(sums.at[pair_to * NX + x_to], arrived.at[me], sums_send, sums_recv, (pair_to, x_to))
        return carry

    lax.fori_loop(1, DEVICES, send_sums, 0)

    reduce_sent(low)
    reduce_sent(high)
    from_last_sent()
    take(arrived, sums_recv)
    sums_out[...] = jnp.sum(arrived[...], axis=0)
    take(relaid, exchange_recv)
    take(new.at[pl.ds(0, DEVICES - 1)], exchange_send)
    take(sums.at[pl.ds(0, DEVICES - 1)], sums_send)


def on_device(vectors, columns, inverse_factor, diagonal, pivots, shell_map):
    vmem = pl.BlockSpec(memory_space=pltpu.VMEM)
    hbm = pl.BlockSpec(memory_space=pl.ANY)
    dma = pltpu.SemaphoreType.DMA
    relaid, diagonal_out, sums = pl.pallas_call(
        kernel,
        out_shape=[
            jax.ShapeDtypeStruct((2, ROWS * DEVICES), F32),
            jax.ShapeDtypeStruct((1, ROWS), F32),
            jax.ShapeDtypeStruct((1, 128), F32),
        ],
        in_specs=[hbm, hbm, vmem, vmem, vmem, vmem],
        out_specs=[hbm, vmem, vmem],
        scratch_shapes=[
            pltpu.VMEM((ROWS, RANK), F32),
            pltpu.VMEM((ROWS, RANK), BF16),
            pltpu.VMEM((ROWS, RANK), BF16),
            pltpu.VMEM((2, ROWS, BATCH), F32),
            pltpu.VMEM((BATCH, WIDE), F32),
            pltpu.VMEM((BATCH, RANK), F32),
            pltpu.VMEM((BATCH, WIDE), F32),
            pltpu.VMEM((BATCH, RANK), F32),
            pltpu.VMEM((BATCH, RANK), BF16),
            pltpu.VMEM((BATCH, RANK), BF16),
            pltpu.VMEM((BATCH, RANK), BF16),
            pltpu.VMEM((BATCH, RANK), BF16),
            pltpu.VMEM((ROWS, BATCH), F32),
            pltpu.VMEM((ROWS, BATCH), F32),
            pltpu.VMEM((DEVICES, 2, ROWS), F32),
            pltpu.VMEM((DEVICES, 1, 128), F32),
            pltpu.VMEM((DEVICES, 1, 128), F32),
            dma((7,)), dma, dma, dma, dma,
            *group_scratch(LOW), *group_scratch(HIGH), *last_scratch(LAST),
        ],
        compiler_params=pltpu.CompilerParams(
            collective_id=0, has_side_effects=True, vmem_limit_bytes=56 << 20
        ),
        name="cholesky",
    )(
        vectors, columns, inverse_factor, diagonal.reshape(1, ROWS), pivots, shell_map.reshape(1, ROWS)
    )
    return relaid, diagonal_out.reshape(ROWS), sums[0, :SHELLS]


def solution(mesh):
    in_specs = (
        P(("pair", "vec"), None),
        P(None, ("pair", "vec"), None),
        P(),
        P(("pair", "vec")),
        P(),
        P(("pair", "vec")),
    )
    out_specs = (P(("pair", "vec"), None), P(("pair", "vec")), P(("pair", "vec")))
    return jax.shard_map(
        on_device, mesh=mesh, in_specs=in_specs, out_specs=out_specs, check_vma=False
    )
```

```python
import functools

import jax
import jax.numpy as jnp
from jax import lax
from jax.experimental import pallas as pl
from jax.experimental.pallas import tpu as pltpu
from jax.sharding import PartitionSpec as P

F32 = jnp.float32
BF16 = jnp.bfloat16
MESH = pl.DeviceIdType.MESH

NZ, NY, NX, NC = 8, 4, 4, 2
BATCH = 256
RANK = 1536
ROWS = 1024
DEVICES = NZ * NY * NX * NC
SHELLS = 64
BLOCK = 512

LOW = (0, 512, 128)
HIGH = (1024, 384, 128)
WIDE = RANK + BATCH
LAST_LOW = (0, 384, 768)
LAST_HIGH = (768, 384, 768)


def split(x):
    high = x.astype(BF16)
    return high, (x - high.astype(F32)).astype(BF16)


def dot_nn(a, b):
    return lax.dot_general(a, b, (((1,), (0,)), ((), ())), preferred_element_type=F32)


def dot_nt(a, b):
    return lax.dot_general(a, b, (((1,), (1,)), ((), ())), preferred_element_type=F32)


def three(dot, a, b):
    return dot(a[0], b[0]) + (dot(a[0], b[1]) + dot(a[1], b[0]))


def times(i, n):
    return pl.multiple_of(i * n, n)


class Group:
    def __init__(self, spec, refs):
        self.first, self.width, self.part = spec
        (self.r0, self.h, self.r1a, self.r1b, self.h2a, self.h2b, self.r2a, self.r2b,
         self.g, self.r3, self.g2, self.send, self.recv) = refs


def group_scratch(spec):
    _, width, part = spec
    return [
        pltpu.VMEM((BATCH, width), F32),
        pltpu.VMEM((BATCH, width), F32),
        pltpu.VMEM((3, 32, width), F32),
        pltpu.VMEM((3, 32, width), F32),
        pltpu.VMEM((32, width), F32),
        pltpu.VMEM((32, width), F32),
        pltpu.VMEM((3, 8, width), F32),
        pltpu.VMEM((3, 8, width), F32),
        pltpu.VMEM((8, 2 * width), F32),
        pltpu.VMEM((NZ - 1, 8, part), F32),
        pltpu.VMEM((8, 2 * width), F32),
        pltpu.SemaphoreType.DMA((12,)),
        pltpu.SemaphoreType.DMA((16,)),
    ]


def last_scratch(spec):
    _, width, _ = spec
    return [
        pltpu.VMEM((32, width), F32),
        pltpu.VMEM((32, width), F32),
        pltpu.VMEM((8, 2 * width), F32),
        pltpu.SemaphoreType.DMA((12,)),
        pltpu.SemaphoreType.DMA((16,)),
    ]


def kernel(
    vectors, columns, factors, diagonal, pivots, shells,
    relaid, diagonal_out, sums_out,
    v32, vh, vl, c32, factor, pick, pick_last, pa, pb, pah, pal, pbh, pbl, ya, yb,
    new, sums, arrived, load_sem, exchange_send, exchange_recv, sums_send, sums_recv,
    *group_refs,
):
    pair = lax.axis_index("pair")
    x = lax.axis_index("vec")
    z, y, c = pair // (NY * NC), (pair // NC) % NY, pair % NC
    me = pair * NX + x
    n = len(group_scratch(LOW))
    low, high = Group(LOW, group_refs[:n]), Group(HIGH, group_refs[n : 2 * n])
    last_low, last_high = (LAST_LOW, *group_refs[2 * n : 2 * n + 5]), (LAST_HIGH, *group_refs[2 * n + 5 :])

    def at(z=z, y=y, x=x, c=c):
        return ((z * NY + y) * NC + c, x)

    def along_x(d):
        return (x + d) % NX

    def along_y(d):
        return (y + d) % NY

    def along_z(d):
        return (z + d) % NZ

    def push(src, dst, send_sem, recv_sem, device):
        pltpu.make_async_remote_copy(
            src_ref=src, dst_ref=dst, send_sem=send_sem, recv_sem=recv_sem,
            device_id=device, device_id_type=MESH,
        ).start()

    def take(ref, sem):
        pltpu.make_async_copy(ref, ref, sem).wait()

    def load(i, width=256):
        at_cols = pl.ds(times(i, width), width)
        return pltpu.make_async_copy(vectors.at[:, at_cols], v32.at[:, at_cols], load_sem.at[i])

    order = [(1 - c) * 2, (1 - c) * 2 + 1, c * 2, c * 2 + 1, 4, 5]
    for i in order:
        load(i).start()
    load_columns = pltpu.make_async_copy(columns, c32, load_sem.at[6])
    load_columns.start()
    load_factors = pltpu.make_async_copy(factors, factor, load_sem.at[7])
    load_factors.start()

    barrier = pltpu.get_barrier_semaphore()

    def greet(device):
        pl.semaphore_signal(barrier, inc=1, device_id=device, device_id_type=MESH)

    greet(at(c=1 - c))
    for d in range(1, 4):
        greet(at(x=along_x(d)))
        greet(at(y=along_y(d)))
    for d in range(1, NZ):
        greet(at(z=along_z(d)))
    root = me == DEVICES - 1
    in_last = z == NZ - 1

    @pl.when(in_last & (c != NC - 1) & ((x == NX - 1) != (y == NY - 1)))
    def _():
        greet(at(z=NZ - 1, y=NY - 1, x=NX - 1, c=NC - 1))

    eye = lax.broadcasted_iota(jnp.int32, (BATCH, BATCH), 0) == lax.broadcasted_iota(jnp.int32, (BATCH, BATCH), 1)
    row = lax.broadcasted_iota(jnp.int32, (BATCH, ROWS), 1) + me * ROWS
    hot = [
        row == jnp.sum(jnp.where(eye, pivots[b : b + 1, :], 0), axis=1, keepdims=True)
        for b in range(2)
    ]
    hot_second = jnp.where(hot[1], 1.0, 0.0).astype(BF16)
    hot_any = jnp.where(hot[0] | hot[1], 1.0, 0.0).astype(BF16)
    kept = jnp.where(root, 0.0, 1.0).astype(F32)

    def gather(i):
        at_cols = pl.ds(times(i, 256), 256)
        load(i).wait()
        vh[:, at_cols], vl[:, at_cols] = split(v32[:, at_cols])
        rows = dot_nn(hot_any, vh[:, at_cols]) + dot_nn(hot_any, vl[:, at_cols])
        pick_last[:, at_cols] = rows
        pick[:, at_cols] = rows * kept

    def half(first, width, core):
        return pl.ds(pl.multiple_of(first + core * width, 128), width)

    def spread(p, g2, first, width, send, recv):
        mine = half(first, width, c)
        rows_a = pl.ds(times(x * NY + y, 8), 8)
        rows_b = pl.ds(pl.multiple_of(128 + (y * NX + x) * 8, 8), 8)
        p[rows_a, mine] = g2[:, :width]
        p[rows_b, mine] = g2[:, width:]
        for d in range(1, 4):
            push(g2.at[:, pl.ds(0, width)], p.at[rows_a, mine], send.at[6], recv.at[6], at(y=along_y(d)))
            push(g2.at[:, pl.ds(width, width)], p.at[rows_b, mine], send.at[6], recv.at[7], at(x=along_x(d)))
        yield
        three_rows = p.at[pl.ds(0, 24), pl.ds(0, width)]
        block_a = p.at[pl.ds(times(x, 32), 32), mine]
        block_b = p.at[pl.ds(pl.multiple_of(128 + y * 32, 32), 32), mine]
        take(three_rows, recv.at[6])
        for d in range(1, 4):
            push(block_a, block_a, send.at[7], recv.at[7 + d], at(x=along_x(d)))
        push(block_a, block_a, send.at[8], recv.at[14], at(c=1 - c))
        take(three_rows, recv.at[7])
        for d in range(1, 4):
            push(block_b, block_b, send.at[7], recv.at[10 + d], at(y=along_y(d)))
        push(block_b, block_b, send.at[8], recv.at[14], at(c=1 - c))
        yield
        for d in range(1, 4):
            block = p.at[pl.ds(times(along_x(4 - d), 32), 32), mine]
            take(block, recv.at[7 + d])
            push(block, block, send.at[8], recv.at[14], at(c=1 - c))
            block = p.at[pl.ds(pl.multiple_of(128 + along_y(4 - d) * 32, 32), 32), mine]
            take(block, recv.at[10 + d])
            push(block, block, send.at[8], recv.at[14], at(c=1 - c))
        yield
        take(p.at[:, pl.ds(0, width)], recv.at[14])

    def spread_sent(p, width, send):
        take(p.at[pl.ds(0, 48), pl.ds(0, width)], send.at[6])
        take(p.at[pl.ds(0, 192), pl.ds(0, width)], send.at[7])
        take(p.at[:, pl.ds(0, width)], send.at[8])

    def reduce(s):
        width, part, send, recv = s.width, s.part, s.send, s.recv
        parts = 2 * width // part
        push(pick.at[:, half(s.first, width, 1 - c)], s.r0, send.at[0], recv.at[0], at(c=1 - c))
        yield
        take(s.r0, recv.at[0])
        s.h[...] = pick[:, half(s.first, width, c)] + s.r0[...]
        for d in range(1, 4):
            to = along_x(d)
            push(s.h.at[pl.ds(times(to, 32), 32)], s.r1a.at[d - 1], send.at[1], recv.at[1], at(x=to))
            to = along_y(d)
            push(s.h.at[pl.ds(pl.multiple_of(128 + to * 32, 32), 32)], s.r1b.at[d - 1], send.at[1], recv.at[2], at(y=to))
        yield
        take(s.r1a, recv.at[1])
        s.h2a[...] = (s.h[pl.ds(times(x, 32), 32), :] + s.r1a[0]) + (s.r1a[1] + s.r1a[2])
        for d in range(1, 4):
            to = along_y(d)
            push(s.h2a.at[pl.ds(times(to, 8), 8)], s.r2a.at[d - 1], send.at[2], recv.at[3], at(y=to))
        take(s.r1b, recv.at[2])
        s.h2b[...] = (s.h[pl.ds(pl.multiple_of(128 + y * 32, 32), 32), :] + s.r1b[0]) + (s.r1b[1] + s.r1b[2])
        for d in range(1, 4):
            to = along_x(d)
            push(s.h2b.at[pl.ds(times(to, 8), 8)], s.r2b.at[d - 1], send.at[2], recv.at[4], at(x=to))
        yield
        take(s.r2a, recv.at[3])
        s.g[:, :width] = (s.h2a[pl.ds(times(y, 8), 8), :] + s.r2a[0]) + (s.r2a[1] + s.r2a[2])
        take(s.r2b, recv.at[4])
        s.g[:, width:] = (s.h2b[pl.ds(times(x, 8), 8), :] + s.r2b[0]) + (s.r2b[1] + s.r2b[2])
        for d in range(1, NZ):
            to = along_z(d)

            @pl.when(to < parts)
            def _():
                push(s.g.at[:, pl.ds(times(to, part), part)], s.r3.at[d - 1], send.at[3], recv.at[5], at(z=to))

        yield
        mine = pl.ds(times(z, part), part)

        @pl.when(z < parts)
        def _():
            take(s.r3, recv.at[5])
            total = s.g[:, mine]
            for d in range(1, NZ):
                total = total + s.r3[d - 1]
            s.g2[:, mine] = total
            for d in range(1, NZ):
                push(s.g2.at[:, mine], s.g2.at[:, mine], send.at[4], recv.at[15], at(z=along_z(d)))

        yield

        @pl.when(z < parts)
        def _():
            take(s.g2.at[:, pl.ds(0, (parts - 1) * part)], recv.at[15])

        @pl.when(z >= parts)
        def _():
            take(s.g2.at[:, pl.ds(0, parts * part)], recv.at[15])

        yield from spread(pa, s.g2, s.first, width, send, recv)

    def reduce_sent(s):
        width, part, send = s.width, s.part, s.send
        parts = 2 * width // part
        take(s.r0, send.at[0])
        take(s.h.at[pl.ds(0, 192)], send.at[1])
        take(s.h.at[pl.ds(0, 48)], send.at[2])

        @pl.when(z < parts)
        def _():
            take(s.g2.at[:, pl.ds(0, (parts - 1) * part)], send.at[3])
            take(s.r3, send.at[4])

        @pl.when(z >= parts)
        def _():
            take(s.g2.at[:, pl.ds(0, parts * part)], send.at[3])

        spread_sent(pa, width, send)

    def from_last(spec, block_a, block_b, g2, send, recv):
        first, width, _ = spec

        @pl.when(root)
        def _():
            block_a[...] = pick_last[pl.ds(times(x, 32), 32), half(first, width, c)]
            block_b[...] = pick_last[pl.ds(pl.multiple_of(128 + y * 32, 32), 32), half(first, width, c)]
            for d in range(4):
                for core in (c, 1 - c) if d else (1 - c,):
                    cols = half(first, width, core)
                    to = along_x(d)
                    push(pick_last.at[pl.ds(times(to, 32), 32), cols], block_a, send.at[0], recv.at[0], at(x=to, c=core))
                    to = along_y(d)
                    push(pick_last.at[pl.ds(pl.multiple_of(128 + to * 32, 32), 32), cols], block_b, send.at[0], recv.at[2], at(y=to, c=core))

        yield

        @pl.when(in_last & (y == NY - 1) & jnp.logical_not(root))
        def _():
            take(block_a, recv.at[0])

        @pl.when(in_last & (y == NY - 1))
        def _():
            for d in range(1, 4):
                to = along_y(d)
                push(block_a.at[pl.ds(times(to, 8), 8)], g2.at[:, pl.ds(0, width)], send.at[2], recv.at[3], at(y=to))
            g2[:, :width] = block_a[pl.ds(times(y, 8), 8), :]

        @pl.when(in_last & (x == NX - 1) & jnp.logical_not(root))
        def _():
            take(block_b, recv.at[2])

        @pl.when(in_last & (x == NX - 1))
        def _():
            for d in range(1, 4):
                to = along_x(d)
                push(block_b.at[pl.ds(times(to, 8), 8)], g2.at[:, pl.ds(width, width)], send.at[3], recv.at[4], at(x=to))
            g2[:, width:] = block_b[pl.ds(times(x, 8), 8), :]

        yield

        @pl.when(in_last & (y != NY - 1))
        def _():
            take(g2.at[:, pl.ds(0, width)], recv.at[3])

        @pl.when(in_last & (x != NX - 1))
        def _():
            take(g2.at[:, pl.ds(width, width)], recv.at[4])

        @pl.when(in_last)
        def _():
            for d in range(1, NZ):
                push(g2, g2, send.at[1], recv.at[1], at(z=along_z(d)))

        yield

        @pl.when(jnp.logical_not(in_last))
        def _():
            take(g2, recv.at[1])

        yield from spread(pb, g2, first, width, send, recv)

    def from_last_sent(spec, block_a, block_b, g2, send, recv):
        _, width, _ = spec

        @pl.when(root)
        def _():
            take(pick_last.at[pl.ds(0, 224), pl.ds(0, 2 * width)], send.at[0])

        @pl.when(in_last & (y == NY - 1))
        def _():
            take(pick_last.at[pl.ds(0, 24), pl.ds(0, width)], send.at[2])

        @pl.when(in_last & (x == NX - 1))
        def _():
            take(pick_last.at[pl.ds(0, 24), pl.ds(0, width)], send.at[3])

        @pl.when(in_last)
        def _():
            take(pick_last.at[pl.ds(0, 56), pl.ds(0, 2 * width)], send.at[1])

        spread_sent(pb, width, send)

    gather(order[0])
    gather(order[1])

    @pl.when(root)
    def _():
        pl.semaphore_wait(barrier, 20)

    @pl.when(jnp.logical_not(root))
    def _():
        pl.semaphore_wait(barrier, 14)

    a, b = reduce(low), reduce(high)
    p, q = from_last(*last_low), from_last(*last_high)

    def go(*streams):
        for stream in streams:
            next(stream, None)

    def times_last(i):
        rows = pl.ds(i * 256, 256)
        yb[rows, :] = three(dot_nt, (vh[rows, :], vl[rows, :]), (pbh[...], pbl[...]))

    def times_other(i, cols):
        rows = pl.ds(i * 256, 256)
        return three(dot_nt, (vh[rows, cols], vl[rows, cols]), (pah[:, cols], pal[:, cols]))

    go(a)
    gather(order[2])
    gather(order[3])
    go(p, a)
    gather(order[4])
    gather(order[5])
    load_columns.wait()
    load_factors.wait()
    own = split(c32[0])
    pick[:, RANK:] = dot_nn(hot_second, own[0]) + dot_nn(hot_second, own[1])
    go(b, q, b, p, a, q, b, p, a, q, b, a, p, b, q, a, p, b, q, a, b, p, q, p)
    low_cols, high_cols = pl.ds(0, RANK // 2), pl.ds(RANK // 2, RANK // 2)
    pbh[:, low_cols], pbl[:, low_cols] = split(pb[:, low_cols])
    go(a, q)
    pbh[:, high_cols], pbl[:, high_cols] = split(pb[:, high_cols])
    times_last(0)
    times_last(1)
    go(b)
    times_last(2)
    times_last(3)

    low_cols, high_cols = pl.ds(0, HIGH[0]), pl.ds(HIGH[0], RANK - HIGH[0])
    f0, f1 = factor[0], factor[1]
    f0_parts = split(f0)
    f0_t, f1_t = split(f0.T), split(f1.T)

    def cross_part(cols):
        return three(dot_nt, (pah[:, cols], pal[:, cols]), (pbh[:, cols], pbl[:, cols]))

    go(a)
    pah[:, low_cols], pal[:, low_cols] = split(pa[:, low_cols])
    for i in range(ROWS // 256):
        ya[pl.ds(i * 256, 256), :] = times_other(i, low_cols)
    cross = cross_part(low_cols)
    go(b)
    pah[:, high_cols], pal[:, high_cols] = split(pa[:, high_cols])
    cross = cross + cross_part(high_cols)
    last_first = jnp.broadcast_to(pivots[0:1, 0:1], (BATCH, BATCH)) >= (DEVICES - 1) * ROWS
    cross = jnp.where(last_first, cross, cross.T)
    pivot_new = three(dot_nn, split(pa[:, RANK:] - cross), f0_parts)
    onto = split(three(dot_nt, f0_parts, split(pivot_new)))
    last_first = jnp.broadcast_to(pivots[0:1, 0:1], (BLOCK, BATCH)) >= (DEVICES - 1) * ROWS

    kinds = DEVICES // 2
    for block in range(ROWS // BLOCK):
        rows = pl.ds(block * BLOCK, BLOCK)
        for i in range(block * BLOCK // 256, (block + 1) * BLOCK // 256):
            ya[pl.ds(i * 256, 256), :] += times_other(i, high_cols)
        y_a, y_b = ya[rows, :], yb[rows, :]
        resid = c32[0, rows, :] - jnp.where(last_first, y_b, y_a)
        parts = split(resid)
        new_first = three(dot_nt, f0_t, parts)
        resid = c32[1, rows, :] - jnp.where(last_first, y_a, y_b) - three(dot_nn, parts, onto)
        new_second = three(dot_nt, f1_t, split(resid))
        new[:kinds, :, rows] = new_first.reshape(kinds, 2, BLOCK)
        new[kinds:, :, rows] = new_second.reshape(kinds, 2, BLOCK)
        diagonal_out[:, rows] = diagonal[:, rows] - jnp.sum(
            new_first * new_first + new_second * new_second, axis=0, keepdims=True
        )
        here = relaid.at[:, pl.ds(pl.multiple_of(me * ROWS + block * BLOCK, BLOCK), BLOCK)]

        def send_new(k, carry):
            y_to, x_to, c_to = (y + k // 4) % NY, (x + k // 16) % NX, (c + k // 64) % NC
            for batch in range(2):
                z_to = batch * (NZ // 2) + (z + k) % (NZ // 2)
                pair_to, x_to = at(z=z_to, y=y_to, x=x_to, c=c_to)
                to = pair_to * NX + x_to
                src = new.at[to, :, rows]

                @pl.when(to == me)
                def _():
                    pltpu.make_async_copy(src, here, exchange_recv).start()

                @pl.when(to != me)
                def _():
                    push(src, here, exchange_send, exchange_recv, (pair_to, x_to))

            return carry

        lax.fori_loop(0, kinds, send_new, 0)

    shell = shells[...]
    hot_device = jnp.where(
        lax.broadcasted_iota(jnp.int32, (DEVICES, ROWS), 0) == shell // SHELLS, 1.0, 0.0
    ).astype(BF16)
    values = jnp.where(
        lax.broadcasted_iota(jnp.int32, (128, ROWS), 0) == shell % SHELLS, diagonal_out[...], 0.0
    )
    first, rest = values.astype(BF16), values
    rest = rest - first.astype(F32)
    second, third = split(rest)
    total = dot_nt(hot_device, first) + (dot_nt(hot_device, second) + dot_nt(hot_device, third))
    sums[...] = total.reshape(DEVICES, 1, 128)
    pltpu.make_async_copy(sums.at[me], arrived.at[me], sums_recv).start()

    def send_sums(k, carry):
        z_to, y_to, x_to, c_to = along_z(k), (y + k // 8) % NY, (x + k // 32) % NX, (c + k // 128) % NC
        pair_to, x_to = at(z=z_to, y=y_to, x=x_to, c=c_to)
        push(sums.at[pair_to * NX + x_to], arrived.at[me], sums_send, sums_recv, (pair_to, x_to))
        return carry

    lax.fori_loop(1, DEVICES, send_sums, 0)

    reduce_sent(low)
    reduce_sent(high)
    from_last_sent(*last_low)
    from_last_sent(*last_high)
    take(arrived, sums_recv)
    sums_out[...] = jnp.sum(arrived[...], axis=0)[:, :SHELLS]
    take(relaid, exchange_recv)
    take(new.at[pl.ds(0, DEVICES - 1)], exchange_send)
    take(sums.at[pl.ds(0, DEVICES - 1)], sums_send)


def on_device(vectors, columns, inverse_factor, diagonal, pivots, shell_map):
    vmem = pl.BlockSpec(memory_space=pltpu.VMEM)
    hbm = pl.BlockSpec(memory_space=pltpu.HBM)
    dma = pltpu.SemaphoreType.DMA
    relaid, diagonal_out, sums = pl.pallas_call(
        kernel,
        out_shape=[
            jax.ShapeDtypeStruct((2, ROWS * DEVICES), F32),
            jax.ShapeDtypeStruct((1, ROWS), F32),
            jax.ShapeDtypeStruct((1, SHELLS), F32),
        ],
        in_specs=[hbm, hbm, hbm, vmem, vmem, vmem],
        out_specs=[pl.BlockSpec(memory_space=pl.ANY), vmem, vmem],
        scratch_shapes=[
            pltpu.VMEM((ROWS, RANK), F32),
            pltpu.VMEM((ROWS, RANK), BF16),
            pltpu.VMEM((ROWS, RANK), BF16),
            pltpu.VMEM((2, ROWS, BATCH), F32),
            pltpu.VMEM((2, BATCH, BATCH), F32),
            pltpu.VMEM((BATCH, WIDE), F32),
            pltpu.VMEM((BATCH, RANK), F32),
            pltpu.VMEM((BATCH, WIDE), F32),
            pltpu.VMEM((BATCH, RANK), F32),
            pltpu.VMEM((BATCH, RANK), BF16),
            pltpu.VMEM((BATCH, RANK), BF16),
            pltpu.VMEM((BATCH, RANK), BF16),
            pltpu.VMEM((BATCH, RANK), BF16),
            pltpu.VMEM((ROWS, BATCH), F32),
            pltpu.VMEM((ROWS, BATCH), F32),
            pltpu.VMEM((DEVICES, 2, ROWS), F32),
            pltpu.VMEM((DEVICES, 1, 128), F32),
            pltpu.VMEM((DEVICES, 1, 128), F32),
            dma((8,)), dma, dma, dma, dma,
            *group_scratch(LOW), *group_scratch(HIGH), *last_scratch(LAST_LOW), *last_scratch(LAST_HIGH),
        ],
        compiler_params=pltpu.CompilerParams(
            collective_id=0, has_side_effects=True, vmem_limit_bytes=60 << 20
        ),
        name="cholesky",
    )(
        vectors, columns, inverse_factor, diagonal.reshape(1, ROWS), pivots, shell_map.reshape(1, ROWS)
    )
    return relaid, diagonal_out.reshape(ROWS), sums.reshape(SHELLS)


def solution(mesh):
    in_specs = (
        P(("pair", "vec"), None),
        P(None, ("pair", "vec"), None),
        P(),
        P(("pair", "vec")),
        P(),
        P(("pair", "vec")),
    )
    out_specs = (P(("pair", "vec"), None), P(("pair", "vec")), P(("pair", "vec")))
    return jax.shard_map(
        on_device, mesh=mesh, in_specs=in_specs, out_specs=out_specs, check_vma=False
    )
```

```python
import functools

import jax
import jax.numpy as jnp
from jax import lax
from jax.experimental import pallas as pl
from jax.experimental.pallas import tpu as pltpu
from jax.sharding import PartitionSpec as P

F32 = jnp.float32
BF16 = jnp.bfloat16
MESH = pl.DeviceIdType.MESH

NZ, NY, NX, NC = 8, 4, 4, 2
BATCH = 256
RANK = 1536
ROWS = 1024
DEVICES = NZ * NY * NX * NC
SHELLS = 64
BLOCKS = ((0, 256), (256, 256), (512, 512))

LOW = (0, 512, 128)
HIGH = (1024, 384, 128)
WIDE = RANK + BATCH
LAST_LOW = (0, 384, 768)
LAST_HIGH = (768, 384, 768)


def split(x):
    high = x.astype(BF16)
    return high, (x - high.astype(F32)).astype(BF16)


def dot_nn(a, b):
    return lax.dot_general(a, b, (((1,), (0,)), ((), ())), preferred_element_type=F32)


def dot_nt(a, b):
    return lax.dot_general(a, b, (((1,), (1,)), ((), ())), preferred_element_type=F32)


def three(dot, a, b):
    return dot(a[0], b[0]) + (dot(a[0], b[1]) + dot(a[1], b[0]))


def times(i, n):
    return pl.multiple_of(i * n, n)


class Group:
    def __init__(self, spec, refs):
        self.first, self.width, self.part = spec
        (self.r0, self.h, self.r1a, self.r1b, self.h2a, self.h2b, self.r2a, self.r2b,
         self.g, self.r3, self.g2, self.send, self.recv) = refs


def group_scratch(spec):
    _, width, part = spec
    return [
        pltpu.VMEM((BATCH, width), F32),
        pltpu.VMEM((BATCH, width), F32),
        pltpu.VMEM((3, 32, width), F32),
        pltpu.VMEM((3, 32, width), F32),
        pltpu.VMEM((32, width), F32),
        pltpu.VMEM((32, width), F32),
        pltpu.VMEM((3, 8, width), F32),
        pltpu.VMEM((3, 8, width), F32),
        pltpu.VMEM((8, 2 * width), F32),
        pltpu.VMEM((NZ - 1, 8, part), F32),
        pltpu.VMEM((8, 2 * width), F32),
        pltpu.SemaphoreType.DMA((12,)),
        pltpu.SemaphoreType.DMA((16,)),
    ]


def last_scratch(spec):
    _, width, _ = spec
    return [
        pltpu.VMEM((32, width), F32),
        pltpu.VMEM((32, width), F32),
        pltpu.VMEM((8, 2 * width), F32),
        pltpu.SemaphoreType.DMA((12,)),
        pltpu.SemaphoreType.DMA((16,)),
    ]


def kernel(
    vectors, columns, factors, diagonal, pivots, shells,
    relaid, diagonal_out, sums_out,
    v32, vh, vl, c32, factor, pick, pick_last, pa, pb, pah, pal, pbh, pbl, ya, yb,
    new, sums, sums_y, sums_plane, sums_z, part_y, part_plane,
    load_sem, exchange_send, exchange_recv, sums_send, sums_recv,
    *group_refs,
):
    pair = lax.axis_index("pair")
    x = lax.axis_index("vec")
    z, y, c = pair // (NY * NC), (pair // NC) % NY, pair % NC
    me = pair * NX + x
    n = len(group_scratch(LOW))
    low, high = Group(LOW, group_refs[:n]), Group(HIGH, group_refs[n : 2 * n])
    last_low, last_high = (LAST_LOW, *group_refs[2 * n : 2 * n + 5]), (LAST_HIGH, *group_refs[2 * n + 5 :])

    def at(z=z, y=y, x=x, c=c):
        return ((z * NY + y) * NC + c, x)

    def along_x(d):
        return (x + d) % NX

    def along_y(d):
        return (y + d) % NY

    def along_z(d):
        return (z + d) % NZ

    def push(src, dst, send_sem, recv_sem, device):
        pltpu.make_async_remote_copy(
            src_ref=src, dst_ref=dst, send_sem=send_sem, recv_sem=recv_sem,
            device_id=device, device_id_type=MESH,
        ).start()

    def take(ref, sem):
        pltpu.make_async_copy(ref, ref, sem).wait()

    def load(i, width=256):
        at_cols = pl.ds(times(i, width), width)
        return pltpu.make_async_copy(vectors.at[:, at_cols], v32.at[:, at_cols], load_sem.at[i])

    order = [(1 - c) * 2, (1 - c) * 2 + 1, c * 2, c * 2 + 1, 4, 5]
    for i in order:
        load(i).start()
    load_columns = pltpu.make_async_copy(columns, c32, load_sem.at[6])
    load_columns.start()
    load_factors = pltpu.make_async_copy(factors, factor, load_sem.at[7])
    load_factors.start()

    barrier = pltpu.get_barrier_semaphore()

    def greet(device):
        pl.semaphore_signal(barrier, inc=1, device_id=device, device_id_type=MESH)

    greet(at(c=1 - c))
    for d in range(1, 4):
        greet(at(x=along_x(d)))
        greet(at(y=along_y(d)))
    for d in range(1, NZ):
        greet(at(z=along_z(d)))
    root = me == DEVICES - 1
    in_last = z == NZ - 1

    @pl.when(in_last & (c != NC - 1) & ((x == NX - 1) != (y == NY - 1)))
    def _():
        greet(at(z=NZ - 1, y=NY - 1, x=NX - 1, c=NC - 1))

    eye = lax.broadcasted_iota(jnp.int32, (BATCH, BATCH), 0) == lax.broadcasted_iota(jnp.int32, (BATCH, BATCH), 1)
    row = lax.broadcasted_iota(jnp.int32, (BATCH, ROWS), 1) + me * ROWS
    hot = [
        row == jnp.sum(jnp.where(eye, pivots[b : b + 1, :], 0), axis=1, keepdims=True)
        for b in range(2)
    ]
    hot_second = jnp.where(hot[1], 1.0, 0.0).astype(BF16)
    hot_any = jnp.where(hot[0] | hot[1], 1.0, 0.0).astype(BF16)
    kept = jnp.where(root, 0.0, 1.0).astype(F32)

    def gather(i):
        at_cols = pl.ds(times(i, 256), 256)
        load(i).wait()
        vh[:, at_cols], vl[:, at_cols] = split(v32[:, at_cols])
        rows = dot_nn(hot_any, vh[:, at_cols]) + dot_nn(hot_any, vl[:, at_cols])
        pick_last[:, at_cols] = rows
        pick[:, at_cols] = rows * kept

    def half(first, width, core):
        return pl.ds(pl.multiple_of(first + core * width, 128), width)

    def spread(p, g2, first, width, send, recv):
        mine = half(first, width, c)
        rows_a = pl.ds(times(x * NY + y, 8), 8)
        rows_b = pl.ds(pl.multiple_of(128 + (y * NX + x) * 8, 8), 8)
        p[rows_a, mine] = g2[:, :width]
        p[rows_b, mine] = g2[:, width:]
        for d in range(1, 4):
            push(g2.at[:, pl.ds(0, width)], p.at[rows_a, mine], send.at[6], recv.at[6], at(y=along_y(d)))
            push(g2.at[:, pl.ds(width, width)], p.at[rows_b, mine], send.at[6], recv.at[7], at(x=along_x(d)))
        yield
        three_rows = p.at[pl.ds(0, 24), pl.ds(0, width)]
        block_a = p.at[pl.ds(times(x, 32), 32), mine]
        block_b = p.at[pl.ds(pl.multiple_of(128 + y * 32, 32), 32), mine]
        take(three_rows, recv.at[6])
        for d in range(1, 4):
            push(block_a, block_a, send.at[7], recv.at[7 + d], at(x=along_x(d)))
        push(block_a, block_a, send.at[8], recv.at[14], at(c=1 - c))
        take(three_rows, recv.at[7])
        for d in range(1, 4):
            push(block_b, block_b, send.at[7], recv.at[10 + d], at(y=along_y(d)))
        push(block_b, block_b, send.at[8], recv.at[14], at(c=1 - c))
        yield
        for d in range(1, 4):
            block = p.at[pl.ds(times(along_x(4 - d), 32), 32), mine]
            take(block, recv.at[7 + d])
            push(block, block, send.at[8], recv.at[14], at(c=1 - c))
            block = p.at[pl.ds(pl.multiple_of(128 + along_y(4 - d) * 32, 32), 32), mine]
            take(block, recv.at[10 + d])
            push(block, block, send.at[8], recv.at[14], at(c=1 - c))
        yield
        take(p.at[:, pl.ds(0, width)], recv.at[14])

    def spread_sent(p, width, send):
        take(p.at[pl.ds(0, 48), pl.ds(0, width)], send.at[6])
        take(p.at[pl.ds(0, 192), pl.ds(0, width)], send.at[7])
        take(p.at[:, pl.ds(0, width)], send.at[8])

    def reduce(s):
        width, part, send, recv = s.width, s.part, s.send, s.recv
        parts = 2 * width // part
        push(pick.at[:, half(s.first, width, 1 - c)], s.r0, send.at[0], recv.at[0], at(c=1 - c))
        yield
        take(s.r0, recv.at[0])
        s.h[...] = pick[:, half(s.first, width, c)] + s.r0[...]
        for d in range(1, 4):
            to = along_x(d)
            push(s.h.at[pl.ds(times(to, 32), 32)], s.r1a.at[d - 1], send.at[1], recv.at[1], at(x=to))
            to = along_y(d)
            push(s.h.at[pl.ds(pl.multiple_of(128 + to * 32, 32), 32)], s.r1b.at[d - 1], send.at[1], recv.at[2], at(y=to))
        yield
        take(s.r1a, recv.at[1])
        s.h2a[...] = (s.h[pl.ds(times(x, 32), 32), :] + s.r1a[0]) + (s.r1a[1] + s.r1a[2])
        for d in range(1, 4):
            to = along_y(d)
            push(s.h2a.at[pl.ds(times(to, 8), 8)], s.r2a.at[d - 1], send.at[2], recv.at[3], at(y=to))
        take(s.r1b, recv.at[2])
        s.h2b[...] = (s.h[pl.ds(pl.multiple_of(128 + y * 32, 32), 32), :] + s.r1b[0]) + (s.r1b[1] + s.r1b[2])
        for d in range(1, 4):
            to = along_x(d)
            push(s.h2b.at[pl.ds(times(to, 8), 8)], s.r2b.at[d - 1], send.at[2], recv.at[4], at(x=to))
        yield
        take(s.r2a, recv.at[3])
        s.g[:, :width] = (s.h2a[pl.ds(times(y, 8), 8), :] + s.r2a[0]) + (s.r2a[1] + s.r2a[2])
        take(s.r2b, recv.at[4])
        s.g[:, width:] = (s.h2b[pl.ds(times(x, 8), 8), :] + s.r2b[0]) + (s.r2b[1] + s.r2b[2])
        for d in range(1, NZ):
            to = along_z(d)

            @pl.when(to < parts)
            def _():
                push(s.g.at[:, pl.ds(times(to, part), part)], s.r3.at[d - 1], send.at[3], recv.at[5], at(z=to))

        yield
        mine = pl.ds(times(z, part), part)

        @pl.when(z < parts)
        def _():
            take(s.r3, recv.at[5])
            total = s.g[:, mine]
            for d in range(1, NZ):
                total = total + s.r3[d - 1]
            s.g2[:, mine] = total
            for d in range(1, NZ):
                push(s.g2.at[:, mine], s.g2.at[:, mine], send.at[4], recv.at[15], at(z=along_z(d)))

        yield

        @pl.when(z < parts)
        def _():
            take(s.g2.at[:, pl.ds(0, (parts - 1) * part)], recv.at[15])

        @pl.when(z >= parts)
        def _():
            take(s.g2.at[:, pl.ds(0, parts * part)], recv.at[15])

        yield from spread(pa, s.g2, s.first, width, send, recv)

    def reduce_sent(s):
        width, part, send = s.width, s.part, s.send
        parts = 2 * width // part
        take(s.r0, send.at[0])
        take(s.h.at[pl.ds(0, 192)], send.at[1])
        take(s.h.at[pl.ds(0, 48)], send.at[2])

        @pl.when(z < parts)
        def _():
            take(s.g2.at[:, pl.ds(0, (parts - 1) * part)], send.at[3])
            take(s.r3, send.at[4])

        @pl.when(z >= parts)
        def _():
            take(s.g2.at[:, pl.ds(0, parts * part)], send.at[3])

        spread_sent(pa, width, send)

    def from_last(spec, block_a, block_b, g2, send, recv):
        first, width, _ = spec

        @pl.when(root)
        def _():
            block_a[...] = pick_last[pl.ds(times(x, 32), 32), half(first, width, c)]
            block_b[...] = pick_last[pl.ds(pl.multiple_of(128 + y * 32, 32), 32), half(first, width, c)]
            for d in range(4):
                for core in (c, 1 - c) if d else (1 - c,):
                    cols = half(first, width, core)
                    to = along_x(d)
                    push(pick_last.at[pl.ds(times(to, 32), 32), cols], block_a, send.at[0], recv.at[0], at(x=to, c=core))
                    to = along_y(d)
                    push(pick_last.at[pl.ds(pl.multiple_of(128 + to * 32, 32), 32), cols], block_b, send.at[0], recv.at[2], at(y=to, c=core))

        yield

        @pl.when(in_last & (y == NY - 1) & jnp.logical_not(root))
        def _():
            take(block_a, recv.at[0])

        @pl.when(in_last & (y == NY - 1))
        def _():
            for d in range(1, 4):
                to = along_y(d)
                push(block_a.at[pl.ds(times(to, 8), 8)], g2.at[:, pl.ds(0, width)], send.at[2], recv.at[3], at(y=to))
            g2[:, :width] = block_a[pl.ds(times(y, 8), 8), :]

        @pl.when(in_last & (x == NX - 1) & jnp.logical_not(root))
        def _():
            take(block_b, recv.at[2])

        @pl.when(in_last & (x == NX - 1))
        def _():
            for d in range(1, 4):
                to = along_x(d)
                push(block_b.at[pl.ds(times(to, 8), 8)], g2.at[:, pl.ds(width, width)], send.at[3], recv.at[4], at(x=to))
            g2[:, width:] = block_b[pl.ds(times(x, 8), 8), :]

        yield

        @pl.when(in_last & (y != NY - 1))
        def _():
            take(g2.at[:, pl.ds(0, width)], recv.at[3])

        @pl.when(in_last & (x != NX - 1))
        def _():
            take(g2.at[:, pl.ds(width, width)], recv.at[4])

        @pl.when(in_last)
        def _():
            for d in range(1, NZ):
                push(g2, g2, send.at[1], recv.at[1], at(z=along_z(d)))

        yield

        @pl.when(jnp.logical_not(in_last))
        def _():
            take(g2, recv.at[1])

        yield from spread(pb, g2, first, width, send, recv)

    def from_last_sent(spec, block_a, block_b, g2, send, recv):
        _, width, _ = spec

        @pl.when(root)
        def _():
            take(pick_last.at[pl.ds(0, 224), pl.ds(0, 2 * width)], send.at[0])

        @pl.when(in_last & (y == NY - 1))
        def _():
            take(pick_last.at[pl.ds(0, 24), pl.ds(0, width)], send.at[2])

        @pl.when(in_last & (x == NX - 1))
        def _():
            take(pick_last.at[pl.ds(0, 24), pl.ds(0, width)], send.at[3])

        @pl.when(in_last)
        def _():
            take(pick_last.at[pl.ds(0, 56), pl.ds(0, 2 * width)], send.at[1])

        spread_sent(pb, width, send)

    for i in order[:5]:
        gather(i)

    @pl.when(root)
    def _():
        pl.semaphore_wait(barrier, 20)

    @pl.when(jnp.logical_not(root))
    def _():
        pl.semaphore_wait(barrier, 14)

    a, b = reduce(low), reduce(high)
    p, q = from_last(*last_low), from_last(*last_high)

    def go(*streams):
        for stream in streams:
            next(stream, None)

    def times_last(i):
        rows = pl.ds(i * 256, 256)
        yb[rows, :] = three(dot_nt, (vh[rows, :], vl[rows, :]), (pbh[...], pbl[...]))

    def times_other(i):
        rows = pl.ds(i * 256, 256)
        return three(dot_nt, (vh[rows, :], vl[rows, :]), (pah[...], pal[...]))

    go(a, p)
    gather(order[5])
    load_columns.wait()
    load_factors.wait()
    own = split(c32[0])
    pick[:, RANK:] = dot_nn(hot_second, own[0]) + dot_nn(hot_second, own[1])
    go(b, a, q, b, p, a, q, b, p, a, q, b, a, p, b, q, a, p, b, q, a, b, p, q, p)
    low_cols, high_cols = pl.ds(0, RANK // 2), pl.ds(RANK // 2, RANK // 2)
    pbh[:, low_cols], pbl[:, low_cols] = split(pb[:, low_cols])
    go(a, q)
    pbh[:, high_cols], pbl[:, high_cols] = split(pb[:, high_cols])
    times_last(0)
    times_last(1)
    go(b)
    times_last(2)
    times_last(3)

    low_cols, high_cols = pl.ds(0, HIGH[0]), pl.ds(HIGH[0], RANK - HIGH[0])
    f0, f1 = factor[0], factor[1]
    f0_parts = split(f0)
    f0_t, f1_t = split(f0.T), split(f1.T)

    def cross_part(cols):
        return three(dot_nt, (pah[:, cols], pal[:, cols]), (pbh[:, cols], pbl[:, cols]))

    go(a)
    pah[:, low_cols], pal[:, low_cols] = split(pa[:, low_cols])
    cross = cross_part(low_cols)
    go(b)
    pah[:, high_cols], pal[:, high_cols] = split(pa[:, high_cols])
    cross = cross + cross_part(high_cols)
    last_first = jnp.broadcast_to(pivots[0:1, 0:1], (BATCH, BATCH)) >= (DEVICES - 1) * ROWS
    cross = jnp.where(last_first, cross, cross.T)
    pivot_new = three(dot_nn, split(pa[:, RANK:] - cross), f0_parts)
    onto = split(three(dot_nt, f0_parts, split(pivot_new)))

    kinds = DEVICES // 2
    half_z = [lax.rem(z + i, NZ // 2) for i in range(NZ // 2)]

    def rest_of(k):
        y_to = lax.rem(y + lax.rem(k, NY), NY)
        x_to = lax.rem(x + lax.rem(lax.div(k, NY), NX), NX)
        c_to = lax.rem(c + lax.div(k, NY * NX), NC)
        return y_to * NC + c_to, x_to

    def shell_steps():
        shell = shells[...]
        device = shell // SHELLS
        place = (device % (NY * NX * NC)) * NZ + device // (NY * NX * NC)
        hot_device = jnp.where(
            lax.broadcasted_iota(jnp.int32, (DEVICES, ROWS), 0) == place, 1.0, 0.0
        ).astype(BF16)
        values = jnp.where(
            lax.broadcasted_iota(jnp.int32, (128, ROWS), 0) == shell % SHELLS, diagonal_out[...], 0.0
        )
        first = values.astype(BF16)
        second, third = split(values - first.astype(F32))
        sums[...] = dot_nt(hot_device, first) + (dot_nt(hot_device, second) + dot_nt(hot_device, third))
        for d in range(1, NY):
            to = along_y(d)
            push(sums.at[pl.ds(times(to, 64), 64)], sums_y.at[d - 1], sums_send.at[0], sums_recv.at[0], at(y=to))
        yield
        take(sums_y, sums_recv.at[0])
        part_y[...] = (sums[pl.ds(times(y, 64), 64), :] + sums_y[0]) + (sums_y[1] + sums_y[2])
        for d in range(1, NX * NC):
            x_to, c_to = along_x(d % NX), lax.rem(c + d // NX, NC)
            push(part_y.at[pl.ds(times(c_to * NX + x_to, 8), 8)], sums_plane.at[d - 1], sums_send.at[1], sums_recv.at[1], at(x=x_to, c=c_to))
        yield
        take(sums_plane, sums_recv.at[1])
        total = part_y[pl.ds(times(c * NX + x, 8), 8), :]
        for d in range(1, NX * NC):
            total = total + sums_plane[d - 1]
        part_plane[...] = total
        for d in range(1, NZ):
            push(part_plane, sums_z.at[d - 1], sums_send.at[2], sums_recv.at[2], at(z=along_z(d)))
        yield
        take(sums_z, sums_recv.at[2])
        total = part_plane[pl.ds(z, 1), :]
        for d in range(1, NZ):
            total = total + sums_z[d - 1, pl.ds(z, 1), :]
        sums_out[...] = total[:, :SHELLS]

    shell = shell_steps()
    for start, count in BLOCKS:
        rows = pl.ds(start, count)
        for i in range(start // 256, (start + count) // 256):
            ya[pl.ds(i * 256, 256), :] = times_other(i)
        y_a, y_b = ya[rows, :], yb[rows, :]
        last_first = jnp.broadcast_to(pivots[0:1, 0:1], (count, BATCH)) >= (DEVICES - 1) * ROWS
        resid = c32[0, rows, :] - jnp.where(last_first, y_b, y_a)
        parts = split(resid)
        new_first = three(dot_nt, f0_t, parts)
        resid = c32[1, rows, :] - jnp.where(last_first, y_a, y_b) - three(dot_nn, parts, onto)
        new_second = three(dot_nt, f1_t, split(resid))
        new[:kinds, :, rows] = new_first.reshape(kinds, 2, count)
        new[kinds:, :, rows] = new_second.reshape(kinds, 2, count)
        diagonal_out[:, rows] = diagonal[:, rows] - jnp.sum(
            new_first * new_first + new_second * new_second, axis=0, keepdims=True
        )
        here = relaid.at[:, pl.ds(pl.multiple_of(me * ROWS + start, 256), count)]

        is_last = start + count == ROWS
        if is_last:
            go(shell)

        def send_new(k, carry):
            pair_rest, x_to = rest_of(k)
            for i in range(NZ // 2):
                for batch in range(2):
                    pair_to = (batch * (NZ // 2) + half_z[i]) * (NY * NC) + pair_rest
                    push(new.at[pair_to * NX + x_to, :, rows], here, exchange_send, exchange_recv, (pair_to, x_to))
            return carry

        for i in range(NZ // 2):
            for batch in range(2):
                z_to = batch * (NZ // 2) + half_z[i]
                src = new.at[at(z=z_to)[0] * NX + x, :, rows]
                if i:
                    push(src, here, exchange_send, exchange_recv, at(z=z_to))
                else:

                    @pl.when(z_to == z)
                    def _():
                        pltpu.make_async_copy(src, here, exchange_recv).start()

                    @pl.when(z_to != z)
                    def _():
                        push(src, here, exchange_send, exchange_recv, at(z=z_to))

        places = NY * NX * NC
        if is_last:
            for a, b in ((1, 11), (11, 21), (21, places)):
                lax.fori_loop(a, b, send_new, 0)
                if b < places:
                    go(shell)
        else:
            lax.fori_loop(1, places, send_new, 0)

    reduce_sent(low)
    reduce_sent(high)
    from_last_sent(*last_low)
    from_last_sent(*last_high)
    go(shell)
    take(relaid, exchange_recv)
    take(new.at[pl.ds(0, DEVICES - 1)], exchange_send)
    take(sums_y, sums_send.at[0])
    take(sums_plane, sums_send.at[1])
    take(sums_z, sums_send.at[2])


def on_device(vectors, columns, inverse_factor, diagonal, pivots, shell_map):
    vmem = pl.BlockSpec(memory_space=pltpu.VMEM)
    hbm = pl.BlockSpec(memory_space=pltpu.HBM)
    dma = pltpu.SemaphoreType.DMA
    relaid, diagonal_out, sums = pl.pallas_call(
        kernel,
        out_shape=[
            jax.ShapeDtypeStruct((2, ROWS * DEVICES), F32),
            jax.ShapeDtypeStruct((1, ROWS), F32),
            jax.ShapeDtypeStruct((1, SHELLS), F32),
        ],
        in_specs=[hbm, hbm, hbm, vmem, vmem, vmem],
        out_specs=[pl.BlockSpec(memory_space=pl.ANY), vmem, vmem],
        scratch_shapes=[
            pltpu.VMEM((ROWS, RANK), F32),
            pltpu.VMEM((ROWS, RANK), BF16),
            pltpu.VMEM((ROWS, RANK), BF16),
            pltpu.VMEM((2, ROWS, BATCH), F32),
            pltpu.VMEM((2, BATCH, BATCH), F32),
            pltpu.VMEM((BATCH, WIDE), F32),
            pltpu.VMEM((BATCH, RANK), F32),
            pltpu.VMEM((BATCH, WIDE), F32),
            pltpu.VMEM((BATCH, RANK), F32),
            pltpu.VMEM((BATCH, RANK), BF16),
            pltpu.VMEM((BATCH, RANK), BF16),
            pltpu.VMEM((BATCH, RANK), BF16),
            pltpu.VMEM((BATCH, RANK), BF16),
            pltpu.VMEM((ROWS, BATCH), F32),
            pltpu.VMEM((ROWS, BATCH), F32),
            pltpu.VMEM((DEVICES, 2, ROWS), F32),
            pltpu.VMEM((DEVICES, 128), F32),
            pltpu.VMEM((NY - 1, 64, 128), F32),
            pltpu.VMEM((NX * NC - 1, 8, 128), F32),
            pltpu.VMEM((NZ - 1, 8, 128), F32),
            pltpu.VMEM((64, 128), F32),
            pltpu.VMEM((8, 128), F32),
            dma((8,)), dma, dma, dma((3,)), dma((3,)),
            *group_scratch(LOW), *group_scratch(HIGH), *last_scratch(LAST_LOW), *last_scratch(LAST_HIGH),
        ],
        compiler_params=pltpu.CompilerParams(
            collective_id=0, has_side_effects=True, vmem_limit_bytes=60 << 20
        ),
        name="cholesky",
    )(
        vectors, columns, inverse_factor, diagonal.reshape(1, ROWS), pivots, shell_map.reshape(1, ROWS)
    )
    return relaid, diagonal_out.reshape(ROWS), sums.reshape(SHELLS)


def solution(mesh):
    in_specs = (
        P(("pair", "vec"), None),
        P(None, ("pair", "vec"), None),
        P(),
        P(("pair", "vec")),
        P(),
        P(("pair", "vec")),
    )
    out_specs = (P(("pair", "vec"), None), P(("pair", "vec")), P(("pair", "vec")))
    return jax.shard_map(
        on_device, mesh=mesh, in_specs=in_specs, out_specs=out_specs, check_vma=False
    )
```

```python
import functools

import jax
import jax.numpy as jnp
from jax import lax
from jax.experimental import pallas as pl
from jax.experimental.pallas import tpu as pltpu
from jax.sharding import PartitionSpec as P

F32 = jnp.float32
BF16 = jnp.bfloat16
MESH = pl.DeviceIdType.MESH

NZ, NY, NX, NC = 8, 4, 4, 2
BATCH = 256
RANK = 1536
ROWS = 1024
DEVICES = NZ * NY * NX * NC
SHELLS = 64
BLOCKS = ((0, 512), (512, 512))

LOW = (0, 512, 128)
HIGH = (1024, 384, 128)
WIDE = RANK + BATCH
LAST_LOW = (0, 384, 768)
LAST_HIGH = (768, 384, 768)


def split(x):
    high = x.astype(BF16)
    return high, (x - high.astype(F32)).astype(BF16)


def dot_nn(a, b):
    return lax.dot_general(a, b, (((1,), (0,)), ((), ())), preferred_element_type=F32)


def dot_nt(a, b):
    return lax.dot_general(a, b, (((1,), (1,)), ((), ())), preferred_element_type=F32)


def three(dot, a, b):
    return dot(a[0], b[0]) + (dot(a[0], b[1]) + dot(a[1], b[0]))


def times(i, n):
    return pl.multiple_of(i * n, n)


class Group:
    def __init__(self, spec, refs):
        self.first, self.width, self.part = spec
        (self.r0, self.h, self.r1a, self.r1b, self.h2a, self.h2b, self.r2a, self.r2b,
         self.g, self.r3, self.g2, self.send, self.recv) = refs


def group_scratch(spec):
    _, width, part = spec
    return [
        pltpu.VMEM((BATCH, width), F32),
        pltpu.VMEM((BATCH, width), F32),
        pltpu.VMEM((3, 32, width), F32),
        pltpu.VMEM((3, 32, width), F32),
        pltpu.VMEM((32, width), F32),
        pltpu.VMEM((32, width), F32),
        pltpu.VMEM((3, 8, width), F32),
        pltpu.VMEM((3, 8, width), F32),
        pltpu.VMEM((8, 2 * width), F32),
        pltpu.VMEM((NZ - 1, 8, part), F32),
        pltpu.VMEM((8, 2 * width), F32),
        pltpu.SemaphoreType.DMA((12,)),
        pltpu.SemaphoreType.DMA((16,)),
    ]


def last_scratch(spec):
    _, width, _ = spec
    return [
        pltpu.VMEM((32, width), F32),
        pltpu.VMEM((32, width), F32),
        pltpu.VMEM((8, 2 * width), F32),
        pltpu.SemaphoreType.DMA((12,)),
        pltpu.SemaphoreType.DMA((16,)),
    ]


def kernel(
    vectors, columns, factors, diagonal, pivots, shells,
    relaid, diagonal_out, sums_out,
    v32, vh, vl, c32, factor, pick, pick_last, pa, pb, pah, pal, pbh, pbl, ya, yb,
    new, sums, sums_y, sums_plane, sums_z, part_y, part_plane,
    load_sem, exchange_send, exchange_recv, sums_send, sums_recv,
    *group_refs,
):
    pair = lax.axis_index("pair")
    x = lax.axis_index("vec")
    z, y, c = pair // (NY * NC), (pair // NC) % NY, pair % NC
    me = pair * NX + x
    n = len(group_scratch(LOW))
    low, high = Group(LOW, group_refs[:n]), Group(HIGH, group_refs[n : 2 * n])
    last_low, last_high = (LAST_LOW, *group_refs[2 * n : 2 * n + 5]), (LAST_HIGH, *group_refs[2 * n + 5 :])

    def at(z=z, y=y, x=x, c=c):
        return ((z * NY + y) * NC + c, x)

    def along_x(d):
        return (x + d) % NX

    def along_y(d):
        return (y + d) % NY

    def along_z(d):
        return (z + d) % NZ

    def push(src, dst, send_sem, recv_sem, device):
        pltpu.make_async_remote_copy(
            src_ref=src, dst_ref=dst, send_sem=send_sem, recv_sem=recv_sem,
            device_id=device, device_id_type=MESH,
        ).start()

    def take(ref, sem):
        pltpu.make_async_copy(ref, ref, sem).wait()

    def load(i, width=256):
        at_cols = pl.ds(times(i, width), width)
        return pltpu.make_async_copy(vectors.at[:, at_cols], v32.at[:, at_cols], load_sem.at[i])

    order = [(1 - c) * 2, (1 - c) * 2 + 1, c * 2, c * 2 + 1, 4, 5]
    for i in order:
        load(i).start()
    load_columns = pltpu.make_async_copy(columns, c32, load_sem.at[6])
    load_columns.start()
    load_factors = pltpu.make_async_copy(factors, factor, load_sem.at[7])
    load_factors.start()

    barrier = pltpu.get_barrier_semaphore()

    def greet(device):
        pl.semaphore_signal(barrier, inc=1, device_id=device, device_id_type=MESH)

    greet(at(c=1 - c))
    for d in range(1, 4):
        greet(at(x=along_x(d)))
        greet(at(y=along_y(d)))
    for d in range(1, NZ):
        greet(at(z=along_z(d)))
    root = me == DEVICES - 1
    in_last = z == NZ - 1

    @pl.when(in_last & (c != NC - 1) & ((x == NX - 1) != (y == NY - 1)))
    def _():
        greet(at(z=NZ - 1, y=NY - 1, x=NX - 1, c=NC - 1))

    eye = lax.broadcasted_iota(jnp.int32, (BATCH, BATCH), 0) == lax.broadcasted_iota(jnp.int32, (BATCH, BATCH), 1)
    row = lax.broadcasted_iota(jnp.int32, (BATCH, ROWS), 1) + me * ROWS
    hot = [
        row == jnp.sum(jnp.where(eye, pivots[b : b + 1, :], 0), axis=1, keepdims=True)
        for b in range(2)
    ]
    hot_second = jnp.where(hot[1], 1.0, 0.0).astype(BF16)
    hot_any = jnp.where(hot[0] | hot[1], 1.0, 0.0).astype(BF16)
    kept = jnp.where(root, 0.0, 1.0).astype(F32)

    def gather(i):
        at_cols = pl.ds(times(i, 256), 256)
        load(i).wait()
        vh[:, at_cols], vl[:, at_cols] = split(v32[:, at_cols])
        rows = dot_nn(hot_any, vh[:, at_cols]) + dot_nn(hot_any, vl[:, at_cols])
        pick_last[:, at_cols] = rows
        pick[:, at_cols] = rows * kept

    def half(first, width, core):
        return pl.ds(pl.multiple_of(first + core * width, 128), width)

    def spread(p, g2, first, width, send, recv):
        mine = half(first, width, c)
        rows_a = pl.ds(times(x * NY + y, 8), 8)
        rows_b = pl.ds(pl.multiple_of(128 + (y * NX + x) * 8, 8), 8)
        p[rows_a, mine] = g2[:, :width]
        p[rows_b, mine] = g2[:, width:]
        for d in range(1, 4):
            push(g2.at[:, pl.ds(0, width)], p.at[rows_a, mine], send.at[6], recv.at[6], at(y=along_y(d)))
            push(g2.at[:, pl.ds(width, width)], p.at[rows_b, mine], send.at[6], recv.at[7], at(x=along_x(d)))
        yield
        three_rows = p.at[pl.ds(0, 24), pl.ds(0, width)]
        block_a = p.at[pl.ds(times(x, 32), 32), mine]
        block_b = p.at[pl.ds(pl.multiple_of(128 + y * 32, 32), 32), mine]
        take(three_rows, recv.at[6])
        for d in range(1, 4):
            push(block_a, block_a, send.at[7], recv.at[7 + d], at(x=along_x(d)))
        push(block_a, block_a, send.at[8], recv.at[14], at(c=1 - c))
        take(three_rows, recv.at[7])
        for d in range(1, 4):
            push(block_b, block_b, send.at[7], recv.at[10 + d], at(y=along_y(d)))
        push(block_b, block_b, send.at[8], recv.at[14], at(c=1 - c))
        yield
        for d in range(1, 4):
            block = p.at[pl.ds(times(along_x(4 - d), 32), 32), mine]
            take(block, recv.at[7 + d])
            push(block, block, send.at[8], recv.at[14], at(c=1 - c))
            block = p.at[pl.ds(pl.multiple_of(128 + along_y(4 - d) * 32, 32), 32), mine]
            take(block, recv.at[10 + d])
            push(block, block, send.at[8], recv.at[14], at(c=1 - c))
        yield
        take(p.at[:, pl.ds(0, width)], recv.at[14])

    def spread_sent(p, width, send):
        take(p.at[pl.ds(0, 48), pl.ds(0, width)], send.at[6])
        take(p.at[pl.ds(0, 192), pl.ds(0, width)], send.at[7])
        take(p.at[:, pl.ds(0, width)], send.at[8])

    def reduce(s):
        width, part, send, recv = s.width, s.part, s.send, s.recv
        parts = 2 * width // part
        push(pick.at[:, half(s.first, width, 1 - c)], s.r0, send.at[0], recv.at[0], at(c=1 - c))
        yield
        take(s.r0, recv.at[0])
        s.h[...] = pick[:, half(s.first, width, c)] + s.r0[...]
        for d in range(1, 4):
            to = along_x(d)
            push(s.h.at[pl.ds(times(to, 32), 32)], s.r1a.at[d - 1], send.at[1], recv.at[1], at(x=to))
            to = along_y(d)
            push(s.h.at[pl.ds(pl.multiple_of(128 + to * 32, 32), 32)], s.r1b.at[d - 1], send.at[1], recv.at[2], at(y=to))
        yield
        take(s.r1a, recv.at[1])
        s.h2a[...] = (s.h[pl.ds(times(x, 32), 32), :] + s.r1a[0]) + (s.r1a[1] + s.r1a[2])
        for d in range(1, 4):
            to = along_y(d)
            push(s.h2a.at[pl.ds(times(to, 8), 8)], s.r2a.at[d - 1], send.at[2], recv.at[3], at(y=to))
        take(s.r1b, recv.at[2])
        s.h2b[...] = (s.h[pl.ds(pl.multiple_of(128 + y * 32, 32), 32), :] + s.r1b[0]) + (s.r1b[1] + s.r1b[2])
        for d in range(1, 4):
            to = along_x(d)
            push(s.h2b.at[pl.ds(times(to, 8), 8)], s.r2b.at[d - 1], send.at[2], recv.at[4], at(x=to))
        yield
        take(s.r2a, recv.at[3])
        s.g[:, :width] = (s.h2a[pl.ds(times(y, 8), 8), :] + s.r2a[0]) + (s.r2a[1] + s.r2a[2])
        take(s.r2b, recv.at[4])
        s.g[:, width:] = (s.h2b[pl.ds(times(x, 8), 8), :] + s.r2b[0]) + (s.r2b[1] + s.r2b[2])
        for d in range(1, NZ):
            to = along_z(d)

            @pl.when(to < parts)
            def _():
                push(s.g.at[:, pl.ds(times(to, part), part)], s.r3.at[d - 1], send.at[3], recv.at[5], at(z=to))

        yield
        mine = pl.ds(times(z, part), part)

        @pl.when(z < parts)
        def _():
            take(s.r3, recv.at[5])
            total = s.g[:, mine]
            for d in range(1, NZ):
                total = total + s.r3[d - 1]
            s.g2[:, mine] = total
            for d in range(1, NZ):
                push(s.g2.at[:, mine], s.g2.at[:, mine], send.at[4], recv.at[15], at(z=along_z(d)))

        yield

        @pl.when(z < parts)
        def _():
            take(s.g2.at[:, pl.ds(0, (parts - 1) * part)], recv.at[15])

        @pl.when(z >= parts)
        def _():
            take(s.g2.at[:, pl.ds(0, parts * part)], recv.at[15])

        yield from spread(pa, s.g2, s.first, width, send, recv)

    def reduce_sent(s):
        width, part, send = s.width, s.part, s.send
        parts = 2 * width // part
        take(s.r0, send.at[0])
        take(s.h.at[pl.ds(0, 192)], send.at[1])
        take(s.h.at[pl.ds(0, 48)], send.at[2])

        @pl.when(z < parts)
        def _():
            take(s.g2.at[:, pl.ds(0, (parts - 1) * part)], send.at[3])
            take(s.r3, send.at[4])

        @pl.when(z >= parts)
        def _():
            take(s.g2.at[:, pl.ds(0, parts * part)], send.at[3])

        spread_sent(pa, width, send)

    def from_last(spec, block_a, block_b, g2, send, recv):
        first, width, _ = spec

        @pl.when(root)
        def _():
            block_a[...] = pick_last[pl.ds(times(x, 32), 32), half(first, width, c)]
            block_b[...] = pick_last[pl.ds(pl.multiple_of(128 + y * 32, 32), 32), half(first, width, c)]
            for d in range(4):
                for core in (c, 1 - c) if d else (1 - c,):
                    cols = half(first, width, core)
                    to = along_x(d)
                    push(pick_last.at[pl.ds(times(to, 32), 32), cols], block_a, send.at[0], recv.at[0], at(x=to, c=core))
                    to = along_y(d)
                    push(pick_last.at[pl.ds(pl.multiple_of(128 + to * 32, 32), 32), cols], block_b, send.at[0], recv.at[2], at(y=to, c=core))

        yield

        @pl.when(in_last & (y == NY - 1) & jnp.logical_not(root))
        def _():
            take(block_a, recv.at[0])

        @pl.when(in_last & (y == NY - 1))
        def _():
            for d in range(1, 4):
                to = along_y(d)
                push(block_a.at[pl.ds(times(to, 8), 8)], g2.at[:, pl.ds(0, width)], send.at[2], recv.at[3], at(y=to))
            g2[:, :width] = block_a[pl.ds(times(y, 8), 8), :]

        @pl.when(in_last & (x == NX - 1) & jnp.logical_not(root))
        def _():
            take(block_b, recv.at[2])

        @pl.when(in_last & (x == NX - 1))
        def _():
            for d in range(1, 4):
                to = along_x(d)
                push(block_b.at[pl.ds(times(to, 8), 8)], g2.at[:, pl.ds(width, width)], send.at[3], recv.at[4], at(x=to))
            g2[:, width:] = block_b[pl.ds(times(x, 8), 8), :]

        yield

        @pl.when(in_last & (y != NY - 1))
        def _():
            take(g2.at[:, pl.ds(0, width)], recv.at[3])

        @pl.when(in_last & (x != NX - 1))
        def _():
            take(g2.at[:, pl.ds(width, width)], recv.at[4])

        @pl.when(in_last)
        def _():
            for d in range(1, NZ):
                push(g2, g2, send.at[1], recv.at[1], at(z=along_z(d)))

        yield

        @pl.when(jnp.logical_not(in_last))
        def _():
            take(g2, recv.at[1])

        yield from spread(pb, g2, first, width, send, recv)

    def from_last_sent(spec, block_a, block_b, g2, send, recv):
        _, width, _ = spec

        @pl.when(root)
        def _():
            take(pick_last.at[pl.ds(0, 224), pl.ds(0, 2 * width)], send.at[0])

        @pl.when(in_last & (y == NY - 1))
        def _():
            take(pick_last.at[pl.ds(0, 24), pl.ds(0, width)], send.at[2])

        @pl.when(in_last & (x == NX - 1))
        def _():
            take(pick_last.at[pl.ds(0, 24), pl.ds(0, width)], send.at[3])

        @pl.when(in_last)
        def _():
            take(pick_last.at[pl.ds(0, 56), pl.ds(0, 2 * width)], send.at[1])

        spread_sent(pb, width, send)

    for i in order[:5]:
        gather(i)

    @pl.when(root)
    def _():
        pl.semaphore_wait(barrier, 20)

    @pl.when(jnp.logical_not(root))
    def _():
        pl.semaphore_wait(barrier, 14)

    a, b = reduce(low), reduce(high)
    p, q = from_last(*last_low), from_last(*last_high)

    def go(*streams):
        for stream in streams:
            next(stream, None)

    def times_last(i):
        rows = pl.ds(i * 256, 256)
        yb[rows, :] = three(dot_nt, (vh[rows, :], vl[rows, :]), (pbh[...], pbl[...]))

    def times_other(i):
        rows = pl.ds(i * 256, 256)
        return three(dot_nt, (vh[rows, :], vl[rows, :]), (pah[...], pal[...]))

    go(a, p)
    gather(order[5])
    load_columns.wait()
    load_factors.wait()
    own = split(c32[0])
    pick[:, RANK:] = dot_nn(hot_second, own[0]) + dot_nn(hot_second, own[1])
    go(b, a, q, b, p, a, q, b, p, a, q, b, a, p, b, q, a, p, b, q, a, b, p, q, p)
    low_cols, high_cols = pl.ds(0, RANK // 2), pl.ds(RANK // 2, RANK // 2)
    pbh[:, low_cols], pbl[:, low_cols] = split(pb[:, low_cols])
    go(a, q)
    pbh[:, high_cols], pbl[:, high_cols] = split(pb[:, high_cols])
    times_last(0)
    go(b)
    for i in range(1, BLOCKS[0][1] // 256):
        times_last(i)

    low_cols, high_cols = pl.ds(0, HIGH[0]), pl.ds(HIGH[0], RANK - HIGH[0])
    f0, f1 = factor[0], factor[1]
    f0_parts = split(f0)
    f0_t, f1_t = split(f0.T), split(f1.T)

    def cross_part(cols):
        return three(dot_nt, (pah[:, cols], pal[:, cols]), (pbh[:, cols], pbl[:, cols]))

    go(a)
    pah[:, low_cols], pal[:, low_cols] = split(pa[:, low_cols])
    cross = cross_part(low_cols)
    go(b)
    pah[:, high_cols], pal[:, high_cols] = split(pa[:, high_cols])
    cross = cross + cross_part(high_cols)
    last_first = jnp.broadcast_to(pivots[0:1, 0:1], (BATCH, BATCH)) >= (DEVICES - 1) * ROWS
    cross = jnp.where(last_first, cross, cross.T)
    pivot_new = three(dot_nn, split(pa[:, RANK:] - cross), f0_parts)
    onto = split(three(dot_nt, f0_parts, split(pivot_new)))

    kinds = DEVICES // 2
    half_z = [lax.rem(z + i, NZ // 2) for i in range(NZ // 2)]

    def rest_of(k):
        y_to = lax.rem(y + lax.rem(k, NY), NY)
        x_to = lax.rem(x + lax.rem(lax.div(k, NY), NX), NX)
        c_to = lax.rem(c + lax.div(k, NY * NX), NC)
        return y_to * NC + c_to, x_to

    def shell_steps():
        shell = shells[...]
        device = shell // SHELLS
        place = (device % (NY * NX * NC)) * NZ + device // (NY * NX * NC)
        hot_device = jnp.where(
            lax.broadcasted_iota(jnp.int32, (DEVICES, ROWS), 0) == place, 1.0, 0.0
        ).astype(BF16)
        values = jnp.where(
            lax.broadcasted_iota(jnp.int32, (128, ROWS), 0) == shell % SHELLS, diagonal_out[...], 0.0
        )
        first = values.astype(BF16)
        second, third = split(values - first.astype(F32))
        sums[...] = dot_nt(hot_device, first) + (dot_nt(hot_device, second) + dot_nt(hot_device, third))
        for d in range(1, NY):
            to = along_y(d)
            push(sums.at[pl.ds(times(to, 64), 64)], sums_y.at[d - 1], sums_send.at[0], sums_recv.at[0], at(y=to))
        yield
        take(sums_y, sums_recv.at[0])
        part_y[...] = (sums[pl.ds(times(y, 64), 64), :] + sums_y[0]) + (sums_y[1] + sums_y[2])
        for d in range(1, NX * NC):
            x_to, c_to = along_x(d % NX), lax.rem(c + d // NX, NC)
            push(part_y.at[pl.ds(times(c_to * NX + x_to, 8), 8)], sums_plane.at[d - 1], sums_send.at[1], sums_recv.at[1], at(x=x_to, c=c_to))
        yield
        take(sums_plane, sums_recv.at[1])
        total = part_y[pl.ds(times(c * NX + x, 8), 8), :]
        for d in range(1, NX * NC):
            total = total + sums_plane[d - 1]
        part_plane[...] = total
        for d in range(1, NZ):
            push(part_plane, sums_z.at[d - 1], sums_send.at[2], sums_recv.at[2], at(z=along_z(d)))
        yield
        take(sums_z, sums_recv.at[2])
        total = part_plane[pl.ds(z, 1), :]
        for d in range(1, NZ):
            total = total + sums_z[d - 1, pl.ds(z, 1), :]
        sums_out[...] = total[:, :SHELLS]

    shell = shell_steps()
    for start, count in BLOCKS:
        rows = pl.ds(start, count)
        for i in range(start // 256, (start + count) // 256):
            if start:
                times_last(i)
            ya[pl.ds(i * 256, 256), :] = times_other(i)
        y_a, y_b = ya[rows, :], yb[rows, :]
        last_first = jnp.broadcast_to(pivots[0:1, 0:1], (count, BATCH)) >= (DEVICES - 1) * ROWS
        resid = c32[0, rows, :] - jnp.where(last_first, y_b, y_a)
        parts = split(resid)
        new_first = three(dot_nt, f0_t, parts)
        resid = c32[1, rows, :] - jnp.where(last_first, y_a, y_b) - three(dot_nn, parts, onto)
        new_second = three(dot_nt, f1_t, split(resid))
        new[:kinds, :, rows] = new_first.reshape(kinds, 2, count)
        new[kinds:, :, rows] = new_second.reshape(kinds, 2, count)
        diagonal_out[:, rows] = diagonal[:, rows] - jnp.sum(
            new_first * new_first + new_second * new_second, axis=0, keepdims=True
        )
        here = relaid.at[:, pl.ds(pl.multiple_of(me * ROWS + start, 256), count)]

        is_last = start + count == ROWS
        if is_last:
            go(shell)

        def send_new(k, carry):
            pair_rest, x_to = rest_of(k)
            for i in range(NZ // 2):
                for batch in range(2):
                    pair_to = (batch * (NZ // 2) + half_z[i]) * (NY * NC) + pair_rest
                    push(new.at[pair_to * NX + x_to, :, rows], here, exchange_send, exchange_recv, (pair_to, x_to))
            return carry

        for i in range(NZ // 2):
            for batch in range(2):
                z_to = batch * (NZ // 2) + half_z[i]
                src = new.at[at(z=z_to)[0] * NX + x, :, rows]
                if i:
                    push(src, here, exchange_send, exchange_recv, at(z=z_to))
                else:

                    @pl.when(z_to == z)
                    def _():
                        pltpu.make_async_copy(src, here, exchange_recv).start()

                    @pl.when(z_to != z)
                    def _():
                        push(src, here, exchange_send, exchange_recv, at(z=z_to))

        places = NY * NX * NC
        if is_last:
            for a, b in ((1, 11), (11, 21), (21, places)):
                lax.fori_loop(a, b, send_new, 0)
                if b < places:
                    go(shell)
        else:
            lax.fori_loop(1, places, send_new, 0)

    reduce_sent(low)
    reduce_sent(high)
    from_last_sent(*last_low)
    from_last_sent(*last_high)
    go(shell)
    take(relaid, exchange_recv)
    take(new.at[pl.ds(0, DEVICES - 1)], exchange_send)
    take(sums_y, sums_send.at[0])
    take(sums_plane, sums_send.at[1])
    take(sums_z, sums_send.at[2])


def on_device(vectors, columns, inverse_factor, diagonal, pivots, shell_map):
    vmem = pl.BlockSpec(memory_space=pltpu.VMEM)
    hbm = pl.BlockSpec(memory_space=pltpu.HBM)
    dma = pltpu.SemaphoreType.DMA
    relaid, diagonal_out, sums = pl.pallas_call(
        kernel,
        out_shape=[
            jax.ShapeDtypeStruct((2, ROWS * DEVICES), F32),
            jax.ShapeDtypeStruct((1, ROWS), F32),
            jax.ShapeDtypeStruct((1, SHELLS), F32),
        ],
        in_specs=[hbm, hbm, hbm, vmem, vmem, vmem],
        out_specs=[pl.BlockSpec(memory_space=pl.ANY), vmem, vmem],
        scratch_shapes=[
            pltpu.VMEM((ROWS, RANK), F32),
            pltpu.VMEM((ROWS, RANK), BF16),
            pltpu.VMEM((ROWS, RANK), BF16),
            pltpu.VMEM((2, ROWS, BATCH), F32),
            pltpu.VMEM((2, BATCH, BATCH), F32),
            pltpu.VMEM((BATCH, WIDE), F32),
            pltpu.VMEM((BATCH, RANK), F32),
            pltpu.VMEM((BATCH, WIDE), F32),
            pltpu.VMEM((BATCH, RANK), F32),
            pltpu.VMEM((BATCH, RANK), BF16),
            pltpu.VMEM((BATCH, RANK), BF16),
            pltpu.VMEM((BATCH, RANK), BF16),
            pltpu.VMEM((BATCH, RANK), BF16),
            pltpu.VMEM((ROWS, BATCH), F32),
            pltpu.VMEM((ROWS, BATCH), F32),
            pltpu.VMEM((DEVICES, 2, ROWS), F32),
            pltpu.VMEM((DEVICES, 128), F32),
            pltpu.VMEM((NY - 1, 64, 128), F32),
            pltpu.VMEM((NX * NC - 1, 8, 128), F32),
            pltpu.VMEM((NZ - 1, 8, 128), F32),
            pltpu.VMEM((64, 128), F32),
            pltpu.VMEM((8, 128), F32),
            dma((8,)), dma, dma, dma((3,)), dma((3,)),
            *group_scratch(LOW), *group_scratch(HIGH), *last_scratch(LAST_LOW), *last_scratch(LAST_HIGH),
        ],
        compiler_params=pltpu.CompilerParams(
            collective_id=0, has_side_effects=True, vmem_limit_bytes=60 << 20
        ),
        name="cholesky",
    )(
        vectors, columns, inverse_factor, diagonal.reshape(1, ROWS), pivots, shell_map.reshape(1, ROWS)
    )
    return relaid, diagonal_out.reshape(ROWS), sums.reshape(SHELLS)


def solution(mesh):
    in_specs = (
        P(("pair", "vec"), None),
        P(None, ("pair", "vec"), None),
        P(),
        P(("pair", "vec")),
        P(),
        P(("pair", "vec")),
    )
    out_specs = (P(("pair", "vec"), None), P(("pair", "vec")), P(("pair", "vec")))
    return jax.shard_map(
        on_device, mesh=mesh, in_specs=in_specs, out_specs=out_specs, check_vma=False
    )
```
